32 devices in a mesh: dp: 8 (over z, core), seq: 4 (over y, x).
Axes of the slice: x: 2, y: 2, z: 4, core: 2. Of those that a mesh axis runs over, the one named last changes fastest.
Arguments:
- queries: bfloat16 [8, 4, 144, 1536], P('dp', 'seq'), may hold values from -32 to 32
- keys: bfloat16 [8, 4, 144, 1536], P('dp', 'seq'), may hold values from -32 to 32
- values: bfloat16 [8, 4, 144, 1536], P('dp', 'seq'), may hold values from -6 to 6
- cotangent: bfloat16 [8, 4, 144, 1536], P('dp', 'seq'), may hold values from -6 to 6
- spatial_count: int32 [8, 4], P('dp', 'seq'), may hold values from 72 to 144, as said below
- clip_ids: int32 [8, 4], P('dp'), may hold values from 0 to 1, never falling along the last dimension, each value on 1 to 3 neighbouring positions
- time_bias: float32 [12, 4], replicated, may hold values from -4 to 4
Outputs:
- attended: bfloat16 [8, 4, 144, 1536], P('dp', 'seq')
- query_grad: bfloat16 [8, 4, 144, 1536], P('dp', 'seq')
- key_grad: bfloat16 [8, 4, 144, 1536], P('dp', 'seq')
- value_grad: bfloat16 [8, 4, 144, 1536], P('dp', 'seq')
- bias_grad: float32 [12, 4], replicated
The draws below stay inside these ranges and needn't reach their ends.
Inputs may be any that keep to these rules, and one draw needn't show every extreme that they name: The live spatial tokens of a frame are its first spatial_count positions; in each group some frame has all 144 live. `clip_ids`: frames of one clip are consecutive; a clip has at most 3 frames.
All inputs are finite; a program needn't handle non-finite values.
Results may differ from the reference program's by a relative error of at most 0.0059.
Values may be sent and summed in bfloat16 or wider, within the bound.
A program may use at most 64 MiB of HBM per device.

```python
import math
import jax
import jax.numpy as jnp
import numpy as np
from jax import lax

HEADS = 12
HEAD = 128
P_SIZE = 144
FR_DEV = 1
CLIPS = 2
GROUPS = 8
FT = 4
N_SEQ = 4


def paired_fields(key):
    full_shape = (GROUPS, FT, P_SIZE, HEADS * HEAD)
    folded = jax.random.fold_in(key, 4057)
    streams = jax.random.split(folded, 2)
    query_field = jnp.clip(jax.random.normal(streams[0], full_shape, jnp.float32), -6.0, 6.0)
    key_field = jnp.clip(jax.random.normal(streams[1], full_shape, jnp.float32), -6.0, 6.0)
    return (query_field, key_field)


def draw_queries(key, part):
    return paired_fields(key)[0].astype(jnp.bfloat16)


def draw_keys(key, part):
    return paired_fields(key)[1].astype(jnp.bfloat16)


def draw_spatial_count(key, part):
    streams = jax.random.split(jax.random.fold_in(key, 313), 2)
    counts = jax.random.randint(streams[0], (GROUPS, FT), P_SIZE // 2, P_SIZE + 1, dtype=jnp.int32)
    full_frame = jax.random.randint(streams[1], (GROUPS, 1), 0, FT, dtype=jnp.int32)
    frame_index = lax.broadcasted_iota(jnp.int32, (GROUPS, FT), 1)
    return jnp.where(frame_index == full_frame, P_SIZE, counts).astype(jnp.int32)


def steps_of(own_key, shape, cuts, least, largest):
    def one(dim, blocks):
        draws = jax.random.uniform(jax.random.fold_in(jax.random.fold_in(own_key, 6), dim), (blocks,), jnp.float32, least / len(cuts), largest / len(cuts))
        return jnp.repeat(jnp.exp(draws), shape[dim] // blocks).reshape((-1,) + (1,) * (len(shape) - dim - 1))

    level = one(*cuts[0])
    for cut in cuts[1:]:
        level = level * one(*cut)
    return level


def profile(amount, total, limit, lean):
    weights = [(1 << 20) // math.isqrt(grade ** lean) + 1 for grade in range(2, amount + 1)]
    rest, holding = total - limit - (amount - 1), [1] * (amount - 1)
    while rest > 0:
        movable = [i for i in range(amount - 1) if holding[i] < limit]
        pool, budget = sum([weights[i] for i in movable]), rest
        for i in movable:
            addition = min(limit - holding[i], max(1, budget * weights[i] // pool), rest)
            holding[i] = holding[i] + addition
            rest = rest - addition
    return np.array([limit] + holding)


def uneven(key, amount, total, bound, lean):
    if amount == 2:
        one = jax.random.randint(key, (), max(1, total - bound), min(bound, total - 1) + 1)
        return jnp.stack([one, total - one])
    tallies = jnp.asarray(profile(amount, total, bound, lean), jnp.int32)
    twos = (amount - 1) // 2
    giver, taker = tallies[1:1 + 2 * twos:2], tallies[2:2 + 2 * twos:2]
    slack = jnp.minimum(giver - 1, bound - taker)
    moved = jax.random.randint(jax.random.fold_in(key, 1), (twos,), 0, 1 << 20) % (slack + 1)
    tallies = tallies.at[1:1 + 2 * twos:2].set(giver - moved).at[2:2 + 2 * twos:2].set(taker + moved)
    return tallies[jax.random.permutation(jax.random.fold_in(key, 2), amount)]


def centred(own_key, shape, scale, limit, cuts=(), kind=jnp.bfloat16):
    values = jax.random.normal(own_key, shape, jnp.float32) * scale
    if len(cuts) > 0:
        values = steps_of(own_key, shape, cuts, -0.22, 0.18) * values
    return jnp.clip(values, min=-limit, max=limit).astype(kind)


def setup_inputs(seed: int = 0) -> dict:
    key_list = jax.random.split(jax.random.key(seed), 8)
    queries = draw_queries(jax.random.fold_in(key_list[7], 71), 0)
    keys = draw_keys(jax.random.fold_in(key_list[7], 71), 0)
    values = centred(key_list[2], (GROUPS, FT, P_SIZE, HEADS * HEAD), 1.0, 6.0, ((0, 8), (1, 4)))
    cotangent = centred(key_list[3], (GROUPS, FT, P_SIZE, HEADS * HEAD), 1.0, 6.0, ((0, 8), (1, 4)))
    spatial_count = draw_spatial_count(jax.random.fold_in(key_list[7], 71), 0)
    clip_ids = jax.vmap(lambda own: jnp.searchsorted(jnp.cumsum(uneven(own, CLIPS, FT, 3 * FR_DEV * N_SEQ // 4, 2)), jnp.arange(FT), side="right"))(jax.random.split(key_list[5], GROUPS)).reshape((GROUPS, FT)).astype(jnp.int32)
    time_bias = centred(key_list[6], (HEADS, FT), 1.0, 4.0, (), jnp.float32)
    return {"queries": queries, "keys": keys, "values": values, "cotangent": cotangent, "spatial_count": spatial_count, "clip_ids": clip_ids, "time_bias": time_bias}


SPACE_PATTERNS = ('bfihe,bfjhe->bfhij', 'bfhij,bfjhe->bfihe', 'bfhij,bfihe->bfjhe')
TIME_PATTERNS = ('biphe,bjphe->bphij', 'bphij,bjphe->biphe', 'bphij,biphe->bjphe')

def split_heads(tensor):
    return tensor.reshape(tensor.shape[:-1] + (HEADS, HEAD)).astype(jnp.float32)

def rounded(tensor):
    return lax.optimization_barrier(tensor.astype(jnp.bfloat16)).astype(jnp.float32)

def attend_pair(patterns, query_part, key_part, value_part, cotangent_part, bias, allowed):
    scaling = 1.0 / math.sqrt(HEAD)
    scores = jnp.einsum(patterns[0], query_part, key_part) * scaling + bias
    scores = jnp.where(allowed, scores, -1e+30)
    row_peak = lax.optimization_barrier(jnp.max(scores, axis=-1, keepdims=True))
    weights = jnp.exp(scores - row_peak)
    shares = weights / lax.optimization_barrier(jnp.sum(weights, axis=-1, keepdims=True))
    shares_half = rounded(shares)
    result = jnp.einsum(patterns[1], shares_half, value_part)
    value_grad = jnp.einsum(patterns[2], shares_half, cotangent_part)
    share_grad = jnp.einsum(patterns[0], cotangent_part, value_part)
    spread = lax.optimization_barrier(jnp.sum(shares * share_grad, axis=-1, keepdims=True))
    score_grad = shares * (share_grad - spread)
    score_half = rounded(score_grad)
    query_grad = jnp.einsum(patterns[1], score_half, key_part) * scaling
    key_grad = jnp.einsum(patterns[2], score_half, query_part) * scaling
    return (result, query_grad, key_grad, value_grad, score_grad)

def reference(queries, keys, values, cotangent, spatial_count, clip_ids, time_bias):
    row_index = lax.broadcasted_iota(jnp.int32, (FT, FT), 0)
    col_index = lax.broadcasted_iota(jnp.int32, (FT, FT), 1)
    distance = jnp.abs(row_index - col_index)
    lag_index = lax.broadcasted_iota(jnp.int32, (FT, FT, FT), 0)
    onehot = (lag_index == distance[None]).astype(jnp.float32)
    bias_table = jnp.tensordot(time_bias, onehot, axes=1, precision=lax.Precision.HIGHEST)[None, None]

    def one_group(pieces):
        query_field, key_field, value_field, cotangent_field, live_count, clip_row = pieces
        query_part = split_heads(query_field[None])
        key_part = split_heads(key_field[None])
        value_part = split_heads(value_field[None])
        cotangent_part = split_heads(cotangent_field[None])
        position = lax.broadcasted_iota(jnp.int32, (1, 1, 1, 1, P_SIZE), 4)
        live_keys = position < live_count.astype(jnp.int32)[None, :, None, None, None]
        space = attend_pair(SPACE_PATTERNS, query_part, key_part, value_part, cotangent_part, 0.0, live_keys)
        same_clip = (clip_row[:, None] == clip_row[None, :])[None, None, None]
        timing = attend_pair(TIME_PATTERNS, query_part, key_part, value_part, cotangent_part, bias_table, same_clip)
        width = HEADS * HEAD
        attended = (space[0] + rounded(timing[0])).astype(jnp.bfloat16).reshape(FT, P_SIZE, width)
        query_grad = (space[1] + rounded(timing[1])).astype(jnp.bfloat16).reshape(FT, P_SIZE, width)
        key_grad = (space[2] + rounded(timing[2])).astype(jnp.bfloat16).reshape(FT, P_SIZE, width)
        value_grad = (space[3] + rounded(timing[3])).astype(jnp.bfloat16).reshape(FT, P_SIZE, width)
        bias_part = jnp.tensordot(lax.optimization_barrier(jnp.sum(timing[4], axis=(0, 1))), onehot, axes=((1, 2), (1, 2)), precision=lax.Precision.HIGHEST)
        return (attended, query_grad, key_grad, value_grad, bias_part)
    outputs = lax.map(one_group, (queries, keys, values, cotangent, spatial_count, clip_ids))
    bias_grad = lax.optimization_barrier(jnp.sum(outputs[4], axis=0)) / math.sqrt(GROUPS * FT * P_SIZE)
    return (outputs[0], outputs[1], outputs[2], outputs[3], bias_grad)
```

```python
import functools
import math

import jax
import jax.numpy as jnp
from jax import lax
from jax.experimental import pallas as pl
from jax.experimental.pallas import tpu as pltpu
from jax.sharding import PartitionSpec as P

SPACE_PATTERNS = ("bfihe,bfjhe->bfhij", "bfhij,bfjhe->bfihe", "bfhij,bfihe->bfjhe")
TIME_PATTERNS = ("biphe,bjphe->bphij", "bphij,bjphe->biphe", "bphij,biphe->bjphe")


def split_heads(tensor, head_count):
    return tensor.reshape(tensor.shape[:-1] + (head_count, tensor.shape[-1] // head_count))


def join_heads(tensor):
    return tensor.reshape(tensor.shape[:-2] + (tensor.shape[-2] * tensor.shape[-1],))


def attend_forward(patterns, query_part, key_part, value_part, bias, allowed):
    scaling = 1.0 / math.sqrt(query_part.shape[-1])
    scores = (
        jnp.einsum(patterns[0], query_part, key_part, preferred_element_type=jnp.float32) * scaling
        + bias
    )
    scores = jnp.where(allowed, scores, -1e30)
    row_peak = jnp.max(scores, axis=-1, keepdims=True)
    weights = jnp.exp(scores - row_peak)
    shares = weights / jnp.sum(weights, axis=-1, keepdims=True)
    shares_half = shares.astype(jnp.bfloat16)
    result = jnp.einsum(patterns[1], shares_half, value_part, preferred_element_type=jnp.float32)
    return (shares, shares_half, result)


def attend_backward(
    patterns, query_part, key_part, value_part, cotangent_part, shares, shares_half
):
    scaling = 1.0 / math.sqrt(query_part.shape[-1])
    value_grad = jnp.einsum(
        patterns[2], shares_half, cotangent_part, preferred_element_type=jnp.float32
    )
    share_grad = jnp.einsum(
        patterns[0], cotangent_part, value_part, preferred_element_type=jnp.float32
    )
    spread = jnp.sum(shares * share_grad, axis=-1, keepdims=True)
    score_grad = shares * (share_grad - spread)
    score_half = score_grad.astype(jnp.bfloat16)
    query_grad = (
        jnp.einsum(patterns[1], score_half, key_part, preferred_element_type=jnp.float32) * scaling
    )
    key_grad = (
        jnp.einsum(patterns[2], score_half, query_part, preferred_element_type=jnp.float32)
        * scaling
    )
    return (query_grad, key_grad, value_grad, score_grad)


def on_device(queries, keys, values, cotangent, spatial_count, clip_ids, time_bias):
    head_count, frames_all = time_bias.shape
    positions = queries.shape[2]
    row_index = lax.broadcasted_iota(jnp.int32, (frames_all, frames_all), 0)
    col_index = lax.broadcasted_iota(jnp.int32, (frames_all, frames_all), 1)
    distance = jnp.abs(row_index - col_index)
    lag_index = lax.broadcasted_iota(jnp.int32, (frames_all, frames_all, frames_all), 0)
    onehot = (lag_index == distance[None]).astype(jnp.float32)
    bias_table = jnp.tensordot(time_bias, onehot, axes=1, precision=lax.Precision.HIGHEST)[
        None, None
    ]
    same_clip = (clip_ids[:, :, None] == clip_ids[:, None, :])[:, None, None]
    position = lax.broadcasted_iota(jnp.int32, (1, 1, 1, 1, positions), 4)
    live_keys = position < spatial_count[:, :, None, None, None]
    space_query = split_heads(queries, head_count)
    space_key = split_heads(keys, head_count)
    space_value = split_heads(values, head_count)
    space_slope = split_heads(cotangent, head_count)
    space_shares, space_half, space_out = attend_forward(
        SPACE_PATTERNS, space_query, space_key, space_value, 0.0, live_keys
    )
    space_grads = attend_backward(
        SPACE_PATTERNS, space_query, space_key, space_value, space_slope, space_shares, space_half
    )
    query_rows, key_rows, value_rows = (
        lax.all_to_all(queries, "seq", split_axis=2, concat_axis=1, tiled=True),
        lax.all_to_all(keys, "seq", split_axis=2, concat_axis=1, tiled=True),
        lax.all_to_all(values, "seq", split_axis=2, concat_axis=1, tiled=True),
    )
    query_part = split_heads(query_rows, head_count)
    key_part = split_heads(key_rows, head_count)
    value_part = split_heads(value_rows, head_count)
    shares, shares_half, result = attend_forward(
        TIME_PATTERNS, query_part, key_part, value_part, bias_table, same_clip
    )
    held = (query_part, key_part, value_part)
    back_out = lax.all_to_all(
        join_heads(result).astype(jnp.bfloat16), "seq", split_axis=1, concat_axis=2, tiled=True
    )
    slope_rows = lax.all_to_all(cotangent, "seq", split_axis=2, concat_axis=1, tiled=True)
    slope_part = split_heads(slope_rows, head_count)
    time_grads = attend_backward(
        TIME_PATTERNS, held[0], held[1], held[2], slope_part, shares, shares_half
    )
    qgrad_rows = join_heads(time_grads[0]).astype(jnp.bfloat16)
    kgrad_rows = join_heads(time_grads[1]).astype(jnp.bfloat16)
    vgrad_rows = join_heads(time_grads[2]).astype(jnp.bfloat16)
    back_query, back_key, back_value = (
        lax.all_to_all(qgrad_rows, "seq", split_axis=1, concat_axis=2, tiled=True),
        lax.all_to_all(kgrad_rows, "seq", split_axis=1, concat_axis=2, tiled=True),
        lax.all_to_all(vgrad_rows, "seq", split_axis=1, concat_axis=2, tiled=True),
    )
    attended = (join_heads(space_out) + back_out.astype(jnp.float32)).astype(jnp.bfloat16)
    query_grad = (join_heads(space_grads[0]) + back_query.astype(jnp.float32)).astype(jnp.bfloat16)
    key_grad = (join_heads(space_grads[1]) + back_key.astype(jnp.float32)).astype(jnp.bfloat16)
    value_grad = (join_heads(space_grads[2]) + back_value.astype(jnp.float32)).astype(jnp.bfloat16)
    bias_part = jnp.tensordot(
        jnp.sum(time_grads[3], axis=(0, 1)),
        onehot,
        axes=((1, 2), (1, 2)),
        precision=lax.Precision.HIGHEST,
    )
    summed = lax.psum(bias_part, ("dp", "seq"))
    bias_grad = summed / math.sqrt(lax.axis_size("dp") * queries.shape[0] * frames_all * positions)
    return (attended, query_grad, key_grad, value_grad, bias_grad)


ROWS = 16
MESH = pl.DeviceIdType.MESH
NT = (((1,), (1,)), ((), ()))
NN = (((1,), (0,)), ((), ()))
TN = (((0,), (0,)), ((), ()))


def dot(left, right, dims):
    return lax.dot_general(left, right, dims, preferred_element_type=jnp.float32)


def attend_block(query, key, value, slope, extra, scaling):
    scores = dot(query, key, NT) * scaling + extra
    share_grad = dot(slope, value, NT)
    weights = jnp.exp(scores - jnp.max(scores, axis=-1, keepdims=True))
    shares = weights * (1.0 / jnp.sum(weights, axis=-1, keepdims=True))
    shares_half = shares.astype(jnp.bfloat16)
    spread = jnp.sum(shares * share_grad, axis=-1, keepdims=True)
    score_grad = shares * (share_grad - spread)
    score_half = score_grad.astype(jnp.bfloat16)
    grads = (
        dot(shares_half, value, NN),
        dot(score_half, key, NN) * scaling,
        dot(score_half, query, TN) * scaling,
        dot(shares_half, slope, TN),
    )
    return grads, score_grad


def partner(count, me, off, back=False):
    if count & (count - 1):
        return lax.rem(me + (count - off if back else off), count)
    other, bit = 0, 1
    while bit < count:
        mine = lax.rem(me // bit, 2)
        other = other + bit * (1 - mine if off & bit else mine)
        bit *= 2
    return other


def kernel(
    dp, n, heads, bias_scale,
    q_ref, k_ref, v_ref, c_ref, count_ref, clip_ref, bias_ref,
    out_ref, qg_ref, kg_ref, vg_ref, bg_ref,
    held, rx, res, ret, space, bx, by,
    load_sem, own_sem, fs, fr, bs, br, xs, xr, ys, yr,
):
    ins = (q_ref, k_ref, v_ref, c_ref)
    outs = (out_ref, qg_ref, kg_ref, vg_ref)
    rows, width = q_ref.shape
    size = width // heads
    per = heads // n
    scaling = 1.0 / math.sqrt(size)
    me = lax.axis_index("seq")
    me_dp = lax.axis_index("dp")

    def cols(index):
        return pl.ds(pl.multiple_of(index * size, size), size)

    def load(a):
        return pltpu.make_async_copy(ins[a], held.at[a], load_sem.at[a])

    def own(a):
        mine = pl.ds(pl.multiple_of(me * per * size, size), per * size)
        return pltpu.make_async_copy(ins[a].at[:, mine], rx.at[a, me], own_sem.at[a])

    def forth(r, a, off, slot):
        to = partner(n, me, off)
        return pltpu.make_async_remote_copy(
            src_ref=ins[a].at[:, cols(to * per + r)],
            dst_ref=rx.at[a, slot, :, cols(r)],
            send_sem=fs.at[r, a, off - 1],
            recv_sem=fr.at[r, a, off - 1],
            device_id={"seq": to},
            device_id_type=MESH,
        )

    def back(r, a, off, slot):
        to = partner(n, me, off)
        return pltpu.make_async_remote_copy(
            src_ref=res.at[a, to, :, cols(r)],
            dst_ref=ret.at[a, :, cols(slot * per + r)],
            send_sem=bs.at[r, a, off - 1],
            recv_sem=br.at[r, a, off - 1],
            device_id={"seq": to},
            device_id_type=MESH,
        )

    def bias_dp(off, slot):
        return pltpu.make_async_remote_copy(
            src_ref=bx.at[me_dp],
            dst_ref=bx.at[slot],
            send_sem=xs.at[off - 1],
            recv_sem=xr.at[off - 1],
            device_id={"dp": partner(dp, me_dp, off)},
            device_id_type=MESH,
        )

    def bias_seq(off, slot):
        return pltpu.make_async_remote_copy(
            src_ref=by.at[me],
            dst_ref=by.at[slot],
            send_sem=ys.at[off - 1],
            recv_sem=yr.at[off - 1],
            device_id={"seq": partner(n, me, off)},
            device_id_type=MESH,
        )

    for a in range(4):
        load(a).start()
        own(a).start()
    barrier = pltpu.get_barrier_semaphore()
    for off in range(1, n):
        pl.semaphore_signal(
            barrier, inc=1, device_id={"seq": partner(n, me, off)}, device_id_type=MESH
        )
    for off in range(1, dp):
        pl.semaphore_signal(
            barrier, inc=1, device_id={"dp": partner(dp, me_dp, off)}, device_id_type=MESH
        )
    pl.semaphore_wait(barrier, n - 1 + dp - 1)

    for r in range(per):
        for a in range(4):
            for off in range(n - 1, 0, -1):
                forth(r, a, off, me).start()

    tokens = n * ROWS
    row = lax.broadcasted_iota(jnp.int32, (tokens, tokens), 0)
    col = lax.broadcasted_iota(jnp.int32, (tokens, tokens), 1)
    row_frame, col_frame = row // ROWS, col // ROWS
    distance = jnp.abs(row_frame - col_frame)
    row_clip = jnp.zeros((tokens, tokens), jnp.int32)
    col_clip = jnp.zeros((tokens, tokens), jnp.int32)
    for f in range(n):
        row_clip = jnp.where(row_frame == f, clip_ref[0, f], row_clip)
        col_clip = jnp.where(col_frame == f, clip_ref[0, f], col_clip)
    allowed = (row_clip == col_clip) & (row - row_frame * ROWS == col - col_frame * ROWS)
    live = lax.broadcasted_iota(jnp.int32, (rows, rows), 1) < count_ref[0, 0]
    space_extra = jnp.where(live, 0.0, -1e30)
    lane = lax.broadcasted_iota(jnp.int32, (8, 128), 1)
    line = lax.broadcasted_iota(jnp.int32, (8, 128), 0)

    for a in range(4):
        load(a).wait()
        own(a).wait()
    bx[me_dp] = jnp.zeros((8, 128), jnp.float32)

    def spatial(h):
        parts = [held[a, :, cols(h)] for a in range(4)]
        grads, _ = attend_block(*parts, space_extra, scaling)
        for a in range(4):
            space[a, :, cols(h)] = grads[a]

    def temporal(r):
        head = me * per + r
        bias = jnp.zeros((tokens, tokens), jnp.float32)
        for d in range(n):
            bias = jnp.where(distance == d, bias_ref[head, d], bias)
        extra = jnp.where(allowed, bias, -1e30)
        total = jnp.zeros((tokens, tokens), jnp.float32)
        for b in range(rows // ROWS):
            span = pl.ds(b * ROWS, ROWS)
            parts = [
                jnp.concatenate([rx[a, f, span, cols(r)] for f in range(n)], axis=0)
                for a in range(4)
            ]
            grads, score_grad = attend_block(*parts, extra, scaling)
            total = total + score_grad
            for a in range(4):
                half = grads[a].astype(jnp.bfloat16)
                for f in range(n):
                    res[a, f, span, cols(r)] = half[f * ROWS : (f + 1) * ROWS]
        tile = bx[me_dp]
        for d in range(n):
            part = jnp.sum(jnp.where(distance == d, total, 0.0), axis=1, keepdims=True)
            part = jnp.sum(part, axis=0, keepdims=True)
            tile = jnp.where((line == r) & (lane == d), part, tile)
        bx[me_dp] = tile

    def step(r, _):
        def pair(i, _):
            for j in range(2):
                spatial(r * n + 2 * i + j)
            return 0

        lax.fori_loop(0, n // 2, pair, 0)
        if n % 2:
            spatial(r * n + n - 1)
        for a in range(4):
            for off in range(1, n):
                forth(r, a, off, partner(n, me, off, True)).wait_recv()
        temporal(r)
        for a in range(4):
            for off in range(n - 1, 0, -1):
                back(r, a, off, me).start()
        return 0

    lax.fori_loop(0, per, step, 0)

    for off in range(1, dp):
        bias_dp(off, me_dp).start()

    def finish(r, _):
        for a in range(4):
            where = cols(me * per + r)
            outs[a][:, where] = (
                space[a, :, where] + res[a, me, :, cols(r)].astype(jnp.float32)
            ).astype(jnp.bfloat16)
        for a in range(4):
            for off in range(1, n):
                source = partner(n, me, off, True)
                back(r, a, off, source).wait_recv()
                where = cols(source * per + r)
                outs[a][:, where] = (
                    space[a, :, where] + ret[a, :, where].astype(jnp.float32)
                ).astype(jnp.bfloat16)
        return 0

    lax.fori_loop(0, per - 1, finish, 0)

    for off in range(1, dp):
        bias_dp(off, partner(dp, me_dp, off, True)).wait_recv()
    summed = bx[0]
    for g in range(1, dp):
        summed = summed + bx[g]
    by[me] = summed * bias_scale
    for off in range(1, n):
        bias_seq(off, me).start()

    finish(per - 1, 0)

    for off in range(1, n):
        bias_seq(off, partner(n, me, off, True)).wait_recv()
    for s in range(n):
        bg_ref[s * per : (s + 1) * per, :] = by[s, 0:per, 0:n]

    def drain(r, _):
        for a in range(4):
            for off in range(1, n):
                forth(r, a, off, me).wait_send()
                back(r, a, off, me).wait_send()
        return 0

    lax.fori_loop(0, per, drain, 0)
    for off in range(1, dp):
        bias_dp(off, me_dp).wait_send()
    for off in range(1, n):
        bias_seq(off, me).wait_send()


def fused(dp, n, queries, keys, values, cotangent, spatial_count, clip_ids, time_bias):
    shape = queries.shape
    rows, width = shape[2:]
    heads = time_bias.shape[0]
    per = heads // n
    flat = jax.ShapeDtypeStruct((rows, width), jnp.bfloat16)
    anywhere = pl.BlockSpec(memory_space=pl.ANY)
    smem = pl.BlockSpec(memory_space=pltpu.SMEM)
    vmem = pl.BlockSpec(memory_space=pltpu.VMEM)
    dma = pltpu.SemaphoreType.DMA
    results = pl.pallas_call(
        functools.partial(kernel, dp, n, heads, 1.0 / math.sqrt(dp * n * rows)),
        out_shape=[flat] * 4 + [jax.ShapeDtypeStruct(time_bias.shape, jnp.float32)],
        in_specs=[anywhere] * 4 + [smem] * 3,
        out_specs=[vmem] * 5,
        scratch_shapes=[
            pltpu.VMEM((4, rows, width), jnp.bfloat16),
            pltpu.VMEM((4, n, rows, width // n), jnp.bfloat16),
            pltpu.VMEM((4, n, rows, width // n), jnp.bfloat16),
            pltpu.VMEM((4, rows, width), jnp.bfloat16),
            pltpu.VMEM((4, rows, width), jnp.float32),
            pltpu.VMEM((dp, 8, 128), jnp.float32),
            pltpu.VMEM((n, 8, 128), jnp.float32),
            dma((4,)),
            dma((4,)),
            dma((per, 4, n - 1)),
            dma((per, 4, n - 1)),
            dma((per, 4, n - 1)),
            dma((per, 4, n - 1)),
            dma((dp - 1,)),
            dma((dp - 1,)),
            dma((n - 1,)),
            dma((n - 1,)),
        ],
        compiler_params=pltpu.CompilerParams(
            collective_id=0, has_side_effects=True, vmem_limit_bytes=40 * 1024 * 1024
        ),
        name="space_time_attention",
    )(
        *(array.reshape(rows, width) for array in (queries, keys, values, cotangent)),
        spatial_count,
        clip_ids,
        time_bias,
    )
    return tuple(array.reshape(shape) for array in results[:4]) + (results[4],)


def on_mesh(dp, n, queries, *rest):
    groups, frames, rows, width = queries.shape
    heads = rest[-1].shape[0]
    fits = groups == 1 and frames == 1 and rows % ROWS == 0 and (width // heads) % 128 == 0
    if fits and n > 1 and dp > 1 and heads % n == 0 and heads // n <= 8 and n <= 8:
        return fused(dp, n, queries, *rest)
    return on_device(queries, *rest)


def solution(mesh):
    return jax.shard_map(
        functools.partial(on_mesh, mesh.shape["dp"], mesh.shape["seq"]),
        mesh=mesh,
        in_specs=(
            P("dp", "seq", None, None),
            P("dp", "seq", None, None),
            P("dp", "seq", None, None),
            P("dp", "seq", None, None),
            P("dp", "seq"),
            P("dp", None),
            P(),
        ),
        out_specs=(
            P("dp", "seq", None, None),
            P("dp", "seq", None, None),
            P("dp", "seq", None, None),
            P("dp", "seq", None, None),
            P(),
        ),
        check_vma=False,
    )
```

```python
import functools
import math

import jax
import jax.numpy as jnp
from jax import lax
from jax.experimental import pallas as pl
from jax.experimental.pallas import tpu as pltpu
from jax.sharding import PartitionSpec as P

SPACE_PATTERNS = ("bfihe,bfjhe->bfhij", "bfhij,bfjhe->bfihe", "bfhij,bfihe->bfjhe")
TIME_PATTERNS = ("biphe,bjphe->bphij", "bphij,bjphe->biphe", "bphij,biphe->bjphe")


def split_heads(tensor, head_count):
    return tensor.reshape(tensor.shape[:-1] + (head_count, tensor.shape[-1] // head_count))


def join_heads(tensor):
    return tensor.reshape(tensor.shape[:-2] + (tensor.shape[-2] * tensor.shape[-1],))


def attend_forward(patterns, query_part, key_part, value_part, bias, allowed):
    scaling = 1.0 / math.sqrt(query_part.shape[-1])
    scores = (
        jnp.einsum(patterns[0], query_part, key_part, preferred_element_type=jnp.float32) * scaling
        + bias
    )
    scores = jnp.where(allowed, scores, -1e30)
    row_peak = jnp.max(scores, axis=-1, keepdims=True)
    weights = jnp.exp(scores - row_peak)
    shares = weights / jnp.sum(weights, axis=-1, keepdims=True)
    shares_half = shares.astype(jnp.bfloat16)
    result = jnp.einsum(patterns[1], shares_half, value_part, preferred_element_type=jnp.float32)
    return (shares, shares_half, result)


def attend_backward(
    patterns, query_part, key_part, value_part, cotangent_part, shares, shares_half
):
    scaling = 1.0 / math.sqrt(query_part.shape[-1])
    value_grad = jnp.einsum(
        patterns[2], shares_half, cotangent_part, preferred_element_type=jnp.float32
    )
    share_grad = jnp.einsum(
        patterns[0], cotangent_part, value_part, preferred_element_type=jnp.float32
    )
    spread = jnp.sum(shares * share_grad, axis=-1, keepdims=True)
    score_grad = shares * (share_grad - spread)
    score_half = score_grad.astype(jnp.bfloat16)
    query_grad = (
        jnp.einsum(patterns[1], score_half, key_part, preferred_element_type=jnp.float32) * scaling
    )
    key_grad = (
        jnp.einsum(patterns[2], score_half, query_part, preferred_element_type=jnp.float32)
        * scaling
    )
    return (query_grad, key_grad, value_grad, score_grad)


def on_device(queries, keys, values, cotangent, spatial_count, clip_ids, time_bias):
    head_count, frames_all = time_bias.shape
    positions = queries.shape[2]
    row_index = lax.broadcasted_iota(jnp.int32, (frames_all, frames_all), 0)
    col_index = lax.broadcasted_iota(jnp.int32, (frames_all, frames_all), 1)
    distance = jnp.abs(row_index - col_index)
    lag_index = lax.broadcasted_iota(jnp.int32, (frames_all, frames_all, frames_all), 0)
    onehot = (lag_index == distance[None]).astype(jnp.float32)
    bias_table = jnp.tensordot(time_bias, onehot, axes=1, precision=lax.Precision.HIGHEST)[
        None, None
    ]
    same_clip = (clip_ids[:, :, None] == clip_ids[:, None, :])[:, None, None]
    position = lax.broadcasted_iota(jnp.int32, (1, 1, 1, 1, positions), 4)
    live_keys = position < spatial_count[:, :, None, None, None]
    space_query = split_heads(queries, head_count)
    space_key = split_heads(keys, head_count)
    space_value = split_heads(values, head_count)
    space_slope = split_heads(cotangent, head_count)
    space_shares, space_half, space_out = attend_forward(
        SPACE_PATTERNS, space_query, space_key, space_value, 0.0, live_keys
    )
    space_grads = attend_backward(
        SPACE_PATTERNS, space_query, space_key, space_value, space_slope, space_shares, space_half
    )
    query_rows, key_rows, value_rows = (
        lax.all_to_all(queries, "seq", split_axis=2, concat_axis=1, tiled=True),
        lax.all_to_all(keys, "seq", split_axis=2, concat_axis=1, tiled=True),
        lax.all_to_all(values, "seq", split_axis=2, concat_axis=1, tiled=True),
    )
    query_part = split_heads(query_rows, head_count)
    key_part = split_heads(key_rows, head_count)
    value_part = split_heads(value_rows, head_count)
    shares, shares_half, result = attend_forward(
        TIME_PATTERNS, query_part, key_part, value_part, bias_table, same_clip
    )
    held = (query_part, key_part, value_part)
    back_out = lax.all_to_all(
        join_heads(result).astype(jnp.bfloat16), "seq", split_axis=1, concat_axis=2, tiled=True
    )
    slope_rows = lax.all_to_all(cotangent, "seq", split_axis=2, concat_axis=1, tiled=True)
    slope_part = split_heads(slope_rows, head_count)
    time_grads = attend_backward(
        TIME_PATTERNS, held[0], held[1], held[2], slope_part, shares, shares_half
    )
    qgrad_rows = join_heads(time_grads[0]).astype(jnp.bfloat16)
    kgrad_rows = join_heads(time_grads[1]).astype(jnp.bfloat16)
    vgrad_rows = join_heads(time_grads[2]).astype(jnp.bfloat16)
    back_query, back_key, back_value = (
        lax.all_to_all(qgrad_rows, "seq", split_axis=1, concat_axis=2, tiled=True),
        lax.all_to_all(kgrad_rows, "seq", split_axis=1, concat_axis=2, tiled=True),
        lax.all_to_all(vgrad_rows, "seq", split_axis=1, concat_axis=2, tiled=True),
    )
    attended = (join_heads(space_out) + back_out.astype(jnp.float32)).astype(jnp.bfloat16)
    query_grad = (join_heads(space_grads[0]) + back_query.astype(jnp.float32)).astype(jnp.bfloat16)
    key_grad = (join_heads(space_grads[1]) + back_key.astype(jnp.float32)).astype(jnp.bfloat16)
    value_grad = (join_heads(space_grads[2]) + back_value.astype(jnp.float32)).astype(jnp.bfloat16)
    bias_part = jnp.tensordot(
        jnp.sum(time_grads[3], axis=(0, 1)),
        onehot,
        axes=((1, 2), (1, 2)),
        precision=lax.Precision.HIGHEST,
    )
    summed = lax.psum(bias_part, ("dp", "seq"))
    bias_grad = summed / math.sqrt(lax.axis_size("dp") * queries.shape[0] * frames_all * positions)
    return (attended, query_grad, key_grad, value_grad, bias_grad)


ROWS = 16
VMEM_BYTES = 60_000_000
MESH = pl.DeviceIdType.MESH
NT = (((1,), (1,)), ((), ()))
NN = (((1,), (0,)), ((), ()))
TN = (((0,), (0,)), ((), ()))


def dot(left, right, dims):
    return lax.dot_general(left, right, dims, preferred_element_type=jnp.float32)


def attend_block(query, key, value, slope, extra, scaling):
    scores = dot(query, key, NT) * scaling + extra
    share_grad = dot(slope, value, NT)
    weights = jnp.exp(scores - jnp.max(scores, axis=-1, keepdims=True))
    shares = weights * (1.0 / jnp.sum(weights, axis=-1, keepdims=True))
    shares_half = shares.astype(jnp.bfloat16)
    spread = jnp.sum(shares * share_grad, axis=-1, keepdims=True)
    score_grad = shares * (share_grad - spread)
    score_half = score_grad.astype(jnp.bfloat16)
    grads = (
        dot(shares_half, value, NN),
        dot(score_half, key, NN) * scaling,
        dot(score_half, query, TN) * scaling,
        dot(shares_half, slope, TN),
    )
    return grads, score_grad


def partner(count, me, off, back=False):
    if count & (count - 1):
        return lax.rem(me + (count - off if back else off), count)
    other, bit = 0, 1
    while bit < count:
        mine = lax.rem(me // bit, 2)
        other = other + bit * (1 - mine if off & bit else mine)
        bit *= 2
    return other


def kernel(
    dp, n, heads, bias_scale,
    q_ref, k_ref, v_ref, c_ref, count_ref, clip_ref, bias_ref,
    out_ref, qg_ref, kg_ref, vg_ref, bg_ref,
    held, rx, res, ret, space, done, bx, by,
    load_sem, own_sem, fs, fr, bs, br, xs, xr, ys, yr, ws,
):
    ins = (q_ref, k_ref, v_ref, c_ref)
    outs = (out_ref, qg_ref, kg_ref, vg_ref)
    rows, width = q_ref.shape
    size = width // heads
    per = heads // n
    scaling = 1.0 / math.sqrt(size)
    me = lax.axis_index("seq")
    me_dp = lax.axis_index("dp")

    def cols(index):
        return pl.ds(pl.multiple_of(index * size, size), size)

    def load(a):
        return pltpu.make_async_copy(ins[a], held.at[a], load_sem.at[a])

    def own(a):
        mine = pl.ds(pl.multiple_of(me * per * size, size), per * size)
        return pltpu.make_async_copy(ins[a].at[:, mine], rx.at[a, me], own_sem.at[a])

    def forth(r, a, off, slot):
        to = partner(n, me, off)
        return pltpu.make_async_remote_copy(
            src_ref=ins[a].at[:, cols(to * per + r)],
            dst_ref=rx.at[a, slot, :, cols(r)],
            send_sem=fs.at[r, a, off - 1],
            recv_sem=fr.at[r, a, off - 1],
            device_id={"seq": to},
            device_id_type=MESH,
        )

    def back(r, a, off, slot):
        to = partner(n, me, off)
        return pltpu.make_async_remote_copy(
            src_ref=res.at[a, to, :, cols(r)],
            dst_ref=ret.at[a, :, cols(slot * per + r)],
            send_sem=bs.at[r, a, off - 1],
            recv_sem=br.at[r, a, off - 1],
            device_id={"seq": to},
            device_id_type=MESH,
        )

    def bias_dp(off, slot):
        return pltpu.make_async_remote_copy(
            src_ref=bx.at[me_dp],
            dst_ref=bx.at[slot],
            send_sem=xs.at[off - 1],
            recv_sem=xr.at[off - 1],
            device_id={"dp": partner(dp, me_dp, off)},
            device_id_type=MESH,
        )

    def bias_seq(off, slot):
        return pltpu.make_async_remote_copy(
            src_ref=by.at[me],
            dst_ref=by.at[slot],
            send_sem=ys.at[off - 1],
            recv_sem=yr.at[off - 1],
            device_id={"seq": partner(n, me, off)},
            device_id_type=MESH,
        )

    for a in range(4):
        load(a).start()
        own(a).start()
    barrier = pltpu.get_barrier_semaphore()
    for off in range(1, n):
        pl.semaphore_signal(
            barrier, inc=1, device_id={"seq": partner(n, me, off)}, device_id_type=MESH
        )
    for off in range(1, dp):
        pl.semaphore_signal(
            barrier, inc=1, device_id={"dp": partner(dp, me_dp, off)}, device_id_type=MESH
        )
    pl.semaphore_wait(barrier, n - 1 + dp - 1)

    def send(r):
        for a in range(4):
            for off in range(n - 1, 0, -1):
                forth(r, a, off, me).start()

    for r in range(min(2, per)):
        send(r)

    tokens = n * ROWS
    row = lax.broadcasted_iota(jnp.int32, (tokens, tokens), 0)
    col = lax.broadcasted_iota(jnp.int32, (tokens, tokens), 1)
    row_frame, col_frame = row // ROWS, col // ROWS
    distance = jnp.abs(row_frame - col_frame)
    row_clip = jnp.zeros((tokens, tokens), jnp.int32)
    col_clip = jnp.zeros((tokens, tokens), jnp.int32)
    for f in range(n):
        row_clip = jnp.where(row_frame == f, clip_ref[0, f], row_clip)
        col_clip = jnp.where(col_frame == f, clip_ref[0, f], col_clip)
    allowed = (row_clip == col_clip) & (row - row_frame * ROWS == col - col_frame * ROWS)
    live = lax.broadcasted_iota(jnp.int32, (rows, rows), 1) < count_ref[0, 0]
    space_extra = jnp.where(live, 0.0, -1e30)
    lane = lax.broadcasted_iota(jnp.int32, (8, 128), 1)
    line = lax.broadcasted_iota(jnp.int32, (8, 128), 0)

    for a in range(4):
        load(a).wait()
        own(a).wait()
    bx[me_dp] = jnp.zeros((8, 128), jnp.float32)

    def spatial(h):
        parts = [held[a, :, cols(h)] for a in range(4)]
        grads, _ = attend_block(*parts, space_extra, scaling)
        for a in range(4):
            space[a, :, cols(h)] = grads[a]

    def temporal(r):
        head = me * per + r
        bias = jnp.zeros((tokens, tokens), jnp.float32)
        for d in range(n):
            bias = jnp.where(distance == d, bias_ref[d, head], bias)
        extra = jnp.where(allowed, bias, -1e30)
        total = jnp.zeros((tokens, tokens), jnp.float32)
        for b in range(rows // ROWS):
            span = pl.ds(b * ROWS, ROWS)
            parts = [
                jnp.concatenate([rx[a, f, span, cols(r)] for f in range(n)], axis=0)
                for a in range(4)
            ]
            grads, score_grad = attend_block(*parts, extra, scaling)
            total = total + score_grad
            for a in range(4):
                half = grads[a].astype(jnp.bfloat16)
                for f in range(n):
                    res[a, f, span, cols(r)] = half[f * ROWS : (f + 1) * ROWS]
        tile = bx[me_dp]
        for d in range(n):
            part = jnp.sum(jnp.where(distance == d, total, 0.0), axis=1, keepdims=True)
            part = jnp.sum(part, axis=0, keepdims=True)
            tile = jnp.where((line == d) & (lane == head), part, tile)
        bx[me_dp] = tile

    def pair(i, _):
        for j in range(2):
            spatial(2 * i + j)
        return 0

    def step(r, _):
        lax.fori_loop(r + 1 - 1 // (r + 1), r + 2, pair, 0)
        for a in range(4):
            for off in range(1, n):
                forth(r, a, off, partner(n, me, off, True)).wait_recv()

        @pl.when(r + 2 < per)
        def _():
            send(r + 2)

        temporal(r)
        for a in range(4):
            for off in range(n - 1, 0, -1):
                back(r, a, off, me).start()
        return 0

    lax.fori_loop(0, per, step, 0)

    for off in range(1, dp):
        bias_dp(off, me_dp).start()

    lax.fori_loop(per + 1, heads // 2, pair, 0)

    def write(r, a, off, source):
        where = cols(source * per + r)
        return pltpu.make_async_copy(
            done.at[a, :, where], outs[a].at[:, where], ws.at[r, a, off]
        )

    def finish(r, _):
        for a in range(4):
            where = cols(me * per + r)
            done[a, :, where] = (
                space[a, :, where] + res[a, me, :, cols(r)].astype(jnp.float32)
            ).astype(jnp.bfloat16)
            write(r, a, 0, me).start()
        for a in range(4):
            for off in range(1, n):
                source = partner(n, me, off, True)
                back(r, a, off, source).wait_recv()
                where = cols(source * per + r)
                done[a, :, where] = (
                    space[a, :, where] + ret[a, :, where].astype(jnp.float32)
                ).astype(jnp.bfloat16)
                write(r, a, off, source).start()
        return 0

    lax.fori_loop(0, per - 1, finish, 0)

    for off in range(1, dp):
        bias_dp(off, partner(dp, me_dp, off, True)).wait_recv()
    summed = bx[0]
    for g in range(1, dp):
        summed = summed + bx[g]
    by[me] = summed * bias_scale
    for off in range(1, n):
        bias_seq(off, me).start()

    finish(per - 1, 0)

    for off in range(1, n):
        bias_seq(off, partner(n, me, off, True)).wait_recv()
    joined = by[0]
    for s in range(1, n):
        joined = joined + by[s]
    bg_ref[...] = joined[0:n, 0:heads]

    def drain(r, _):
        for a in range(4):
            for off in range(1, n):
                forth(r, a, off, me).wait_send()
                back(r, a, off, me).wait_send()
                write(r, a, off, partner(n, me, off, True)).wait()
            write(r, a, 0, me).wait()
        return 0

    lax.fori_loop(0, per, drain, 0)
    for off in range(1, dp):
        bias_dp(off, me_dp).wait_send()
    for off in range(1, n):
        bias_seq(off, me).wait_send()


def hand_over(*refs):
    count = len(refs) // 2
    copies = []
    for i in range(count):
        rows = refs[i].shape[0]
        cuts = 3 if rows % (3 * ROWS) == 0 else 1
        for cut in range(cuts):
            part = pl.ds(cut * rows // cuts, rows // cuts)
            copies.append(
                pltpu.make_async_copy(
                    refs[i].at[part], refs[count + i].at[part], refs[-1].at[i, cut]
                )
            )
    for copy in copies:
        copy.start()
    for copy in copies:
        copy.wait()


def fused(dp, n, queries, keys, values, cotangent, spatial_count, clip_ids, time_bias):
    shape = queries.shape
    rows, width = shape[2:]
    heads = time_bias.shape[0]
    per = heads // n
    flat = jax.ShapeDtypeStruct((rows, width), jnp.bfloat16)
    hbm = pl.BlockSpec(memory_space=pltpu.HBM)
    smem = pl.BlockSpec(memory_space=pltpu.SMEM)
    vmem = pl.BlockSpec(memory_space=pltpu.VMEM)
    dma = pltpu.SemaphoreType.DMA
    shapes = [flat] * 4 + [jax.ShapeDtypeStruct((n, heads), jnp.float32)]
    results = pl.pallas_call(
        functools.partial(kernel, dp, n, heads, 1.0 / math.sqrt(dp * n * rows)),
        out_shape=shapes,
        in_specs=[hbm] * 4 + [smem] * 3,
        out_specs=[hbm] * 4 + [vmem],
        scratch_shapes=[
            pltpu.VMEM((4, rows, width), jnp.bfloat16),
            pltpu.VMEM((4, n, rows, width // n), jnp.bfloat16),
            pltpu.VMEM((4, n, rows, width // n), jnp.bfloat16),
            pltpu.VMEM((4, rows, width), jnp.bfloat16),
            pltpu.VMEM((4, rows, width), jnp.float32),
            pltpu.VMEM((4, rows, width), jnp.bfloat16),
            pltpu.VMEM((dp, 8, 128), jnp.float32),
            pltpu.VMEM((n, 8, 128), jnp.float32),
            dma((4,)),
            dma((4,)),
            dma((per, 4, n - 1)),
            dma((per, 4, n - 1)),
            dma((per, 4, n - 1)),
            dma((per, 4, n - 1)),
            dma((dp - 1,)),
            dma((dp - 1,)),
            dma((n - 1,)),
            dma((n - 1,)),
            dma((per, 4, n)),
        ],
        compiler_params=pltpu.CompilerParams(
            collective_id=0, has_side_effects=True, vmem_limit_bytes=VMEM_BYTES
        ),
        name="space_time_attention",
    )(
        *(array.reshape(rows, width) for array in (queries, keys, values, cotangent)),
        spatial_count,
        clip_ids,
        time_bias.T,
    )
    results = pl.pallas_call(
        hand_over,
        out_shape=shapes,
        in_specs=[hbm] * 5,
        out_specs=[hbm] * 5,
        scratch_shapes=[dma((5, 3))],
        compiler_params=pltpu.CompilerParams(vmem_limit_bytes=VMEM_BYTES),
        name="hand_over",
    )(*results)
    return tuple(array.reshape(shape) for array in results[:4]) + (results[4].T,)


def on_mesh(dp, n, queries, *rest):
    groups, frames, rows, width = queries.shape
    heads = rest[-1].shape[0]
    fits = groups == 1 and frames == 1 and rows % ROWS == 0 and (width // heads) % 128 == 0
    if fits and heads <= 128 and n > 1 and dp > 1 and heads % n == 0 and heads % 2 == 0 and heads // n < heads // 2 and n <= 8:
        return fused(dp, n, queries, *rest)
    return on_device(queries, *rest)


def solution(mesh):
    return jax.shard_map(
        functools.partial(on_mesh, mesh.shape["dp"], mesh.shape["seq"]),
        mesh=mesh,
        in_specs=(
            P("dp", "seq", None, None),
            P("dp", "seq", None, None),
            P("dp", "seq", None, None),
            P("dp", "seq", None, None),
            P("dp", "seq"),
            P("dp", None),
            P(),
        ),
        out_specs=(
            P("dp", "seq", None, None),
            P("dp", "seq", None, None),
            P("dp", "seq", None, None),
            P("dp", "seq", None, None),
            P(),
        ),
        check_vma=False,
    )
```

```python
import functools
import math

import jax
import jax.numpy as jnp
from jax import lax
from jax.experimental import pallas as pl
from jax.experimental.pallas import tpu as pltpu
from jax.sharding import PartitionSpec as P

SPACE_PATTERNS = ("bfihe,bfjhe->bfhij", "bfhij,bfjhe->bfihe", "bfhij,bfihe->bfjhe")
TIME_PATTERNS = ("biphe,bjphe->bphij", "bphij,bjphe->biphe", "bphij,biphe->bjphe")


def split_heads(tensor, head_count):
    return tensor.reshape(tensor.shape[:-1] + (head_count, tensor.shape[-1] // head_count))


def join_heads(tensor):
    return tensor.reshape(tensor.shape[:-2] + (tensor.shape[-2] * tensor.shape[-1],))


def attend_forward(patterns, query_part, key_part, value_part, bias, allowed):
    scaling = 1.0 / math.sqrt(query_part.shape[-1])
    scores = (
        jnp.einsum(patterns[0], query_part, key_part, preferred_element_type=jnp.float32) * scaling
        + bias
    )
    scores = jnp.where(allowed, scores, -1e30)
    row_peak = jnp.max(scores, axis=-1, keepdims=True)
    weights = jnp.exp(scores - row_peak)
    shares = weights / jnp.sum(weights, axis=-1, keepdims=True)
    shares_half = shares.astype(jnp.bfloat16)
    result = jnp.einsum(patterns[1], shares_half, value_part, preferred_element_type=jnp.float32)
    return (shares, shares_half, result)


def attend_backward(
    patterns, query_part, key_part, value_part, cotangent_part, shares, shares_half
):
    scaling = 1.0 / math.sqrt(query_part.shape[-1])
    value_grad = jnp.einsum(
        patterns[2], shares_half, cotangent_part, preferred_element_type=jnp.float32
    )
    share_grad = jnp.einsum(
        patterns[0], cotangent_part, value_part, preferred_element_type=jnp.float32
    )
    spread = jnp.sum(shares * share_grad, axis=-1, keepdims=True)
    score_grad = shares * (share_grad - spread)
    score_half = score_grad.astype(jnp.bfloat16)
    query_grad = (
        jnp.einsum(patterns[1], score_half, key_part, preferred_element_type=jnp.float32) * scaling
    )
    key_grad = (
        jnp.einsum(patterns[2], score_half, query_part, preferred_element_type=jnp.float32)
        * scaling
    )
    return (query_grad, key_grad, value_grad, score_grad)


def on_device(queries, keys, values, cotangent, spatial_count, clip_ids, time_bias):
    head_count, frames_all = time_bias.shape
    positions = queries.shape[2]
    row_index = lax.broadcasted_iota(jnp.int32, (frames_all, frames_all), 0)
    col_index = lax.broadcasted_iota(jnp.int32, (frames_all, frames_all), 1)
    distance = jnp.abs(row_index - col_index)
    lag_index = lax.broadcasted_iota(jnp.int32, (frames_all, frames_all, frames_all), 0)
    onehot = (lag_index == distance[None]).astype(jnp.float32)
    bias_table = jnp.tensordot(time_bias, onehot, axes=1, precision=lax.Precision.HIGHEST)[
        None, None
    ]
    same_clip = (clip_ids[:, :, None] == clip_ids[:, None, :])[:, None, None]
    position = lax.broadcasted_iota(jnp.int32, (1, 1, 1, 1, positions), 4)
    live_keys = position < spatial_count[:, :, None, None, None]
    space_query = split_heads(queries, head_count)
    space_key = split_heads(keys, head_count)
    space_value = split_heads(values, head_count)
    space_slope = split_heads(cotangent, head_count)
    space_shares, space_half, space_out = attend_forward(
        SPACE_PATTERNS, space_query, space_key, space_value, 0.0, live_keys
    )
    space_grads = attend_backward(
        SPACE_PATTERNS, space_query, space_key, space_value, space_slope, space_shares, space_half
    )
    query_rows, key_rows, value_rows = (
        lax.all_to_all(queries, "seq", split_axis=2, concat_axis=1, tiled=True),
        lax.all_to_all(keys, "seq", split_axis=2, concat_axis=1, tiled=True),
        lax.all_to_all(values, "seq", split_axis=2, concat_axis=1, tiled=True),
    )
    query_part = split_heads(query_rows, head_count)
    key_part = split_heads(key_rows, head_count)
    value_part = split_heads(value_rows, head_count)
    shares, shares_half, result = attend_forward(
        TIME_PATTERNS, query_part, key_part, value_part, bias_table, same_clip
    )
    held = (query_part, key_part, value_part)
    back_out = lax.all_to_all(
        join_heads(result).astype(jnp.bfloat16), "seq", split_axis=1, concat_axis=2, tiled=True
    )
    slope_rows = lax.all_to_all(cotangent, "seq", split_axis=2, concat_axis=1, tiled=True)
    slope_part = split_heads(slope_rows, head_count)
    time_grads = attend_backward(
        TIME_PATTERNS, held[0], held[1], held[2], slope_part, shares, shares_half
    )
    qgrad_rows = join_heads(time_grads[0]).astype(jnp.bfloat16)
    kgrad_rows = join_heads(time_grads[1]).astype(jnp.bfloat16)
    vgrad_rows = join_heads(time_grads[2]).astype(jnp.bfloat16)
    back_query, back_key, back_value = (
        lax.all_to_all(qgrad_rows, "seq", split_axis=1, concat_axis=2, tiled=True),
        lax.all_to_all(kgrad_rows, "seq", split_axis=1, concat_axis=2, tiled=True),
        lax.all_to_all(vgrad_rows, "seq", split_axis=1, concat_axis=2, tiled=True),
    )
    attended = (join_heads(space_out) + back_out.astype(jnp.float32)).astype(jnp.bfloat16)
    query_grad = (join_heads(space_grads[0]) + back_query.astype(jnp.float32)).astype(jnp.bfloat16)
    key_grad = (join_heads(space_grads[1]) + back_key.astype(jnp.float32)).astype(jnp.bfloat16)
    value_grad = (join_heads(space_grads[2]) + back_value.astype(jnp.float32)).astype(jnp.bfloat16)
    bias_part = jnp.tensordot(
        jnp.sum(time_grads[3], axis=(0, 1)),
        onehot,
        axes=((1, 2), (1, 2)),
        precision=lax.Precision.HIGHEST,
    )
    summed = lax.psum(bias_part, ("dp", "seq"))
    bias_grad = summed / math.sqrt(lax.axis_size("dp") * queries.shape[0] * frames_all * positions)
    return (attended, query_grad, key_grad, value_grad, bias_grad)


ROWS = 16
VMEM_BYTES = 60_000_000
MESH = pl.DeviceIdType.MESH
NT = (((1,), (1,)), ((), ()))
NN = (((1,), (0,)), ((), ()))
TN = (((0,), (0,)), ((), ()))


def dot(left, right, dims):
    return lax.dot_general(left, right, dims, preferred_element_type=jnp.float32)


def attend_block(query, key, value, slope, extra, scaling):
    scores = dot(query, key, NT) * scaling + extra
    share_grad = dot(slope, value, NT)
    weights = jnp.exp(scores - jnp.max(scores, axis=-1, keepdims=True))
    shares = weights * (1.0 / jnp.sum(weights, axis=-1, keepdims=True))
    shares_half = shares.astype(jnp.bfloat16)
    spread = jnp.sum(shares * share_grad, axis=-1, keepdims=True)
    score_grad = shares * (share_grad - spread)
    score_half = score_grad.astype(jnp.bfloat16)
    grads = (
        dot(shares_half, value, NN),
        dot(score_half, key, NN) * scaling,
        dot(score_half, query, TN) * scaling,
        dot(shares_half, slope, TN),
    )
    return grads, score_grad


def partner(count, me, off, back=False):
    if count & (count - 1):
        return lax.rem(me + (count - off if back else off), count)
    other, bit = 0, 1
    while bit < count:
        mine = lax.rem(me // bit, 2)
        other = other + bit * (1 - mine if off & bit else mine)
        bit *= 2
    return other


def kernel(
    dp, n, heads, bias_scale,
    q_ref, k_ref, v_ref, c_ref, count_ref, clip_ref, bias_ref,
    out_ref, qg_ref, kg_ref, vg_ref, bg_ref,
    held, rx, res, ret, space, done, bx, by,
    load_sem, own_sem, fs, fr, bs, br, xs, xr, ys, yr, ws,
):
    ins = (q_ref, k_ref, v_ref, c_ref)
    outs = (out_ref, qg_ref, kg_ref, vg_ref)
    rows, width = q_ref.shape
    size = width // heads
    per = heads // n
    scaling = 1.0 / math.sqrt(size)
    me = lax.axis_index("seq")
    me_dp = lax.axis_index("dp")

    def cols(index):
        return pl.ds(pl.multiple_of(index * size, size), size)

    def load(a):
        return pltpu.make_async_copy(ins[a], held.at[a], load_sem.at[a])

    def own(a):
        mine = pl.ds(pl.multiple_of(me * per * size, size), per * size)
        return pltpu.make_async_copy(ins[a].at[:, mine], rx.at[a, me], own_sem.at[a])

    def forth(r, a, off, slot):
        to = partner(n, me, off)
        return pltpu.make_async_remote_copy(
            src_ref=ins[a].at[:, cols(to * per + r)],
            dst_ref=rx.at[a, slot, :, cols(r)],
            send_sem=fs.at[r, a, off - 1],
            recv_sem=fr.at[r, a, off - 1],
            device_id={"seq": to},
            device_id_type=MESH,
        )

    def back(r, a, off, slot):
        to = partner(n, me, off)
        return pltpu.make_async_remote_copy(
            src_ref=res.at[a, to, :, cols(r)],
            dst_ref=ret.at[a, :, cols(slot * per + r)],
            send_sem=bs.at[r, a, off - 1],
            recv_sem=br.at[r, a, off - 1],
            device_id={"seq": to},
            device_id_type=MESH,
        )

    def bias_dp(off, slot):
        return pltpu.make_async_remote_copy(
            src_ref=bx.at[me_dp],
            dst_ref=bx.at[slot],
            send_sem=xs.at[off - 1],
            recv_sem=xr.at[off - 1],
            device_id={"dp": partner(dp, me_dp, off)},
            device_id_type=MESH,
        )

    def bias_seq(off, slot):
        return pltpu.make_async_remote_copy(
            src_ref=by.at[me],
            dst_ref=by.at[slot],
            send_sem=ys.at[off - 1],
            recv_sem=yr.at[off - 1],
            device_id={"seq": partner(n, me, off)},
            device_id_type=MESH,
        )

    for a in range(4):
        load(a).start()
        own(a).start()
    barrier = pltpu.get_barrier_semaphore()
    for off in range(1, n):
        pl.semaphore_signal(
            barrier, inc=1, device_id={"seq": partner(n, me, off)}, device_id_type=MESH
        )
    for off in range(1, dp):
        pl.semaphore_signal(
            barrier, inc=1, device_id={"dp": partner(dp, me_dp, off)}, device_id_type=MESH
        )
    pl.semaphore_wait(barrier, n - 1 + dp - 1)

    def send(r):
        for a in range(4):
            for off in range(n - 1, 0, -1):
                forth(r, a, off, me).start()

    for r in range(min(2, per)):
        send(r)

    tokens = n * ROWS
    row = lax.broadcasted_iota(jnp.int32, (tokens, tokens), 0)
    col = lax.broadcasted_iota(jnp.int32, (tokens, tokens), 1)
    row_frame, col_frame = row // ROWS, col // ROWS
    distance = jnp.abs(row_frame - col_frame)
    row_clip = jnp.zeros((tokens, tokens), jnp.int32)
    col_clip = jnp.zeros((tokens, tokens), jnp.int32)
    for f in range(n):
        row_clip = jnp.where(row_frame == f, clip_ref[0, f], row_clip)
        col_clip = jnp.where(col_frame == f, clip_ref[0, f], col_clip)
    allowed = (row_clip == col_clip) & (row - row_frame * ROWS == col - col_frame * ROWS)
    live = lax.broadcasted_iota(jnp.int32, (rows, rows), 1) < count_ref[0, 0]
    space_extra = jnp.where(live, 0.0, -1e30)
    lane = lax.broadcasted_iota(jnp.int32, (8, 128), 1)
    line = lax.broadcasted_iota(jnp.int32, (8, 128), 0)

    for a in range(4):
        load(a).wait()
        own(a).wait()
    bx[me_dp] = jnp.zeros((8, 128), jnp.float32)

    def spatial(h):
        parts = [held[a, :, cols(h)] for a in range(4)]
        grads, _ = attend_block(*parts, space_extra, scaling)
        for a in range(4):
            space[a, :, cols(h)] = grads[a]

    def temporal(r):
        head = me * per + r
        bias = jnp.zeros((tokens, tokens), jnp.float32)
        for d in range(n):
            bias = jnp.where(distance == d, bias_ref[d, head], bias)
        extra = jnp.where(allowed, bias, -1e30)
        total = jnp.zeros((tokens, tokens), jnp.float32)
        for b in range(rows // ROWS):
            span = pl.ds(b * ROWS, ROWS)
            parts = [
                jnp.concatenate([rx[a, f, span, cols(r)] for f in range(n)], axis=0)
                for a in range(4)
            ]
            grads, score_grad = attend_block(*parts, extra, scaling)
            total = total + score_grad
            for a in range(4):
                half = grads[a].astype(jnp.bfloat16)
                for f in range(n):
                    res[a, f, span, cols(r)] = half[f * ROWS : (f + 1) * ROWS]
        tile = bx[me_dp]
        for d in range(n):
            part = jnp.sum(jnp.where(distance == d, total, 0.0), axis=1, keepdims=True)
            part = jnp.sum(part, axis=0, keepdims=True)
            tile = jnp.where((line == d) & (lane == head), part, tile)
        bx[me_dp] = tile

    def pair(i, _):
        for j in range(2):
            spatial(2 * i + j)
        return 0

    def step(r, _):
        lax.fori_loop(r + 1 - 1 // (r + 1), r + 2, pair, 0)
        for a in range(4):
            for off in range(1, n):
                forth(r, a, off, partner(n, me, off, True)).wait_recv()

        @pl.when(r + 2 < per)
        def _():
            send(r + 2)

        temporal(r)
        for a in range(4):
            for off in range(n - 1, 0, -1):
                back(r, a, off, me).start()
        return 0

    lax.fori_loop(0, per, step, 0)

    for off in range(1, dp):
        bias_dp(off, me_dp).start()

    lax.fori_loop(per + 1, heads // 2, pair, 0)

    def write(r, a, off, source):
        where = cols(source * per + r)
        return pltpu.make_async_copy(
            done.at[a, :, where], outs[a].at[:, where], ws.at[r, a, off]
        )

    def finish(r, _):
        for a in range(4):
            where = cols(me * per + r)
            done[a, :, where] = (
                space[a, :, where] + res[a, me, :, cols(r)].astype(jnp.float32)
            ).astype(jnp.bfloat16)
            write(r, a, 0, me).start()
        for a in range(4):
            for off in range(1, n):
                source = partner(n, me, off, True)
                back(r, a, off, source).wait_recv()
                where = cols(source * per + r)
                done[a, :, where] = (
                    space[a, :, where] + ret[a, :, where].astype(jnp.float32)
                ).astype(jnp.bfloat16)
                write(r, a, off, source).start()
        return 0

    lax.fori_loop(0, per - 1, finish, 0)

    for off in range(1, dp):
        bias_dp(off, partner(dp, me_dp, off, True)).wait_recv()
    summed = bx[0]
    for g in range(1, dp):
        summed = summed + bx[g]
    by[me] = summed * bias_scale
    for off in range(1, n):
        bias_seq(off, me).start()

    finish(per - 1, 0)

    for off in range(1, n):
        bias_seq(off, partner(n, me, off, True)).wait_recv()
    joined = by[0]
    for s in range(1, n):
        joined = joined + by[s]
    bg_ref[...] = joined[0:n, 0:heads]

    def drain(r, _):
        for a in range(4):
            for off in range(1, n):
                forth(r, a, off, me).wait_send()
                back(r, a, off, me).wait_send()
                write(r, a, off, partner(n, me, off, True)).wait()
            write(r, a, 0, me).wait()
        return 0

    lax.fori_loop(0, per, drain, 0)
    for off in range(1, dp):
        bias_dp(off, me_dp).wait_send()
    for off in range(1, n):
        bias_seq(off, me).wait_send()


def hand_over(*refs):
    count = (len(refs) - 2) // 3
    sources, targets, stages = refs[:count], refs[count : 2 * count], refs[2 * count : 3 * count]
    into_sem, out_sem = refs[3 * count :]
    into, out = [], []
    for i in range(count):
        rows = sources[i].shape[0]
        cuts = 3 if rows % (3 * ROWS) == 0 else 1
        for cut in range(cuts):
            part = pl.ds(cut * rows // cuts, rows // cuts)
            stage = stages[i].at[part]
            into.append(pltpu.make_async_copy(sources[i].at[part], stage, into_sem.at[i, cut]))
            out.append(pltpu.make_async_copy(stage, targets[i].at[part], out_sem.at[i, cut]))
    for copy in into:
        copy.start()
    for here, there in zip(into, out):
        here.wait()
        there.start()
    for copy in out:
        copy.wait()


def fused(dp, n, queries, keys, values, cotangent, spatial_count, clip_ids, time_bias):
    shape = queries.shape
    rows, width = shape[2:]
    heads = time_bias.shape[0]
    per = heads // n
    flat = jax.ShapeDtypeStruct((rows, width), jnp.bfloat16)
    hbm = pl.BlockSpec(memory_space=pltpu.HBM)
    smem = pl.BlockSpec(memory_space=pltpu.SMEM)
    vmem = pl.BlockSpec(memory_space=pltpu.VMEM)
    dma = pltpu.SemaphoreType.DMA
    shapes = [flat] * 4 + [jax.ShapeDtypeStruct((n, heads), jnp.float32)]
    results = pl.pallas_call(
        functools.partial(kernel, dp, n, heads, 1.0 / math.sqrt(dp * n * rows)),
        out_shape=shapes,
        in_specs=[hbm] * 4 + [smem] * 3,
        out_specs=[hbm] * 4 + [vmem],
        scratch_shapes=[
            pltpu.VMEM((4, rows, width), jnp.bfloat16),
            pltpu.VMEM((4, n, rows, width // n), jnp.bfloat16),
            pltpu.VMEM((4, n, rows, width // n), jnp.bfloat16),
            pltpu.VMEM((4, rows, width), jnp.bfloat16),
            pltpu.VMEM((4, rows, width), jnp.float32),
            pltpu.VMEM((4, rows, width), jnp.bfloat16),
            pltpu.VMEM((dp, 8, 128), jnp.float32),
            pltpu.VMEM((n, 8, 128), jnp.float32),
            dma((4,)),
            dma((4,)),
            dma((per, 4, n - 1)),
            dma((per, 4, n - 1)),
            dma((per, 4, n - 1)),
            dma((per, 4, n - 1)),
            dma((dp - 1,)),
            dma((dp - 1,)),
            dma((n - 1,)),
            dma((n - 1,)),
            dma((per, 4, n)),
        ],
        compiler_params=pltpu.CompilerParams(
            collective_id=0, has_side_effects=True, vmem_limit_bytes=VMEM_BYTES
        ),
        name="space_time_attention",
    )(
        *(array.reshape(rows, width) for array in (queries, keys, values, cotangent)),
        spatial_count,
        clip_ids,
        time_bias.T,
    )
    results = pl.pallas_call(
        hand_over,
        out_shape=shapes,
        in_specs=[hbm] * 5,
        out_specs=[hbm] * 5,
        scratch_shapes=[pltpu.VMEM(kind.shape, kind.dtype) for kind in shapes]
        + [dma((5, 3)), dma((5, 3))],
        compiler_params=pltpu.CompilerParams(vmem_limit_bytes=VMEM_BYTES),
        name="hand_over",
    )(*results)
    return tuple(array.reshape(shape) for array in results[:4]) + (results[4].T,)


def on_mesh(dp, n, queries, *rest):
    groups, frames, rows, width = queries.shape
    heads = rest[-1].shape[0]
    fits = groups == 1 and frames == 1 and rows % ROWS == 0 and (width // heads) % 128 == 0
    if fits and heads <= 128 and n > 1 and dp > 1 and heads % n == 0 and heads % 2 == 0 and heads // n < heads // 2 and n <= 8:
        return fused(dp, n, queries, *rest)
    return on_device(queries, *rest)


def solution(mesh):
    return jax.shard_map(
        functools.partial(on_mesh, mesh.shape["dp"], mesh.shape["seq"]),
        mesh=mesh,
        in_specs=(
            P("dp", "seq", None, None),
            P("dp", "seq", None, None),
            P("dp", "seq", None, None),
            P("dp", "seq", None, None),
            P("dp", "seq"),
            P("dp", None),
            P(),
        ),
        out_specs=(
            P("dp", "seq", None, None),
            P("dp", "seq", None, None),
            P("dp", "seq", None, None),
            P("dp", "seq", None, None),
            P(),
        ),
        check_vma=False,
    )
```

```python
import functools
import math

import jax
import jax.numpy as jnp
from jax import lax
from jax.experimental import pallas as pl
from jax.experimental.pallas import tpu as pltpu
from jax.sharding import PartitionSpec as P

SPACE_PATTERNS = ("bfihe,bfjhe->bfhij", "bfhij,bfjhe->bfihe", "bfhij,bfihe->bfjhe")
TIME_PATTERNS = ("biphe,bjphe->bphij", "bphij,bjphe->biphe", "bphij,biphe->bjphe")


def split_heads(tensor, head_count):
    return tensor.reshape(tensor.shape[:-1] + (head_count, tensor.shape[-1] // head_count))


def join_heads(tensor):
    return tensor.reshape(tensor.shape[:-2] + (tensor.shape[-2] * tensor.shape[-1],))


def attend_forward(patterns, query_part, key_part, value_part, bias, allowed):
    scaling = 1.0 / math.sqrt(query_part.shape[-1])
    scores = (
        jnp.einsum(patterns[0], query_part, key_part, preferred_element_type=jnp.float32) * scaling
        + bias
    )
    scores = jnp.where(allowed, scores, -1e30)
    row_peak = jnp.max(scores, axis=-1, keepdims=True)
    weights = jnp.exp(scores - row_peak)
    shares = weights / jnp.sum(weights, axis=-1, keepdims=True)
    shares_half = shares.astype(jnp.bfloat16)
    result = jnp.einsum(patterns[1], shares_half, value_part, preferred_element_type=jnp.float32)
    return (shares, shares_half, result)


def attend_backward(
    patterns, query_part, key_part, value_part, cotangent_part, shares, shares_half
):
    scaling = 1.0 / math.sqrt(query_part.shape[-1])
    value_grad = jnp.einsum(
        patterns[2], shares_half, cotangent_part, preferred_element_type=jnp.float32
    )
    share_grad = jnp.einsum(
        patterns[0], cotangent_part, value_part, preferred_element_type=jnp.float32
    )
    spread = jnp.sum(shares * share_grad, axis=-1, keepdims=True)
    score_grad = shares * (share_grad - spread)
    score_half = score_grad.astype(jnp.bfloat16)
    query_grad = (
        jnp.einsum(patterns[1], score_half, key_part, preferred_element_type=jnp.float32) * scaling
    )
    key_grad = (
        jnp.einsum(patterns[2], score_half, query_part, preferred_element_type=jnp.float32)
        * scaling
    )
    return (query_grad, key_grad, value_grad, score_grad)


def on_device(queries, keys, values, cotangent, spatial_count, clip_ids, time_bias):
    head_count, frames_all = time_bias.shape
    positions = queries.shape[2]
    row_index = lax.broadcasted_iota(jnp.int32, (frames_all, frames_all), 0)
    col_index = lax.broadcasted_iota(jnp.int32, (frames_all, frames_all), 1)
    distance = jnp.abs(row_index - col_index)
    lag_index = lax.broadcasted_iota(jnp.int32, (frames_all, frames_all, frames_all), 0)
    onehot = (lag_index == distance[None]).astype(jnp.float32)
    bias_table = jnp.tensordot(time_bias, onehot, axes=1, precision=lax.Precision.HIGHEST)[
        None, None
    ]
    same_clip = (clip_ids[:, :, None] == clip_ids[:, None, :])[:, None, None]
    position = lax.broadcasted_iota(jnp.int32, (1, 1, 1, 1, positions), 4)
    live_keys = position < spatial_count[:, :, None, None, None]
    space_query = split_heads(queries, head_count)
    space_key = split_heads(keys, head_count)
    space_value = split_heads(values, head_count)
    space_slope = split_heads(cotangent, head_count)
    space_shares, space_half, space_out = attend_forward(
        SPACE_PATTERNS, space_query, space_key, space_value, 0.0, live_keys
    )
    space_grads = attend_backward(
        SPACE_PATTERNS, space_query, space_key, space_value, space_slope, space_shares, space_half
    )
    query_rows, key_rows, value_rows = (
        lax.all_to_all(queries, "seq", split_axis=2, concat_axis=1, tiled=True),
        lax.all_to_all(keys, "seq", split_axis=2, concat_axis=1, tiled=True),
        lax.all_to_all(values, "seq", split_axis=2, concat_axis=1, tiled=True),
    )
    query_part = split_heads(query_rows, head_count)
    key_part = split_heads(key_rows, head_count)
    value_part = split_heads(value_rows, head_count)
    shares, shares_half, result = attend_forward(
        TIME_PATTERNS, query_part, key_part, value_part, bias_table, same_clip
    )
    held = (query_part, key_part, value_part)
    back_out = lax.all_to_all(
        join_heads(result).astype(jnp.bfloat16), "seq", split_axis=1, concat_axis=2, tiled=True
    )
    slope_rows = lax.all_to_all(cotangent, "seq", split_axis=2, concat_axis=1, tiled=True)
    slope_part = split_heads(slope_rows, head_count)
    time_grads = attend_backward(
        TIME_PATTERNS, held[0], held[1], held[2], slope_part, shares, shares_half
    )
    qgrad_rows = join_heads(time_grads[0]).astype(jnp.bfloat16)
    kgrad_rows = join_heads(time_grads[1]).astype(jnp.bfloat16)
    vgrad_rows = join_heads(time_grads[2]).astype(jnp.bfloat16)
    back_query, back_key, back_value = (
        lax.all_to_all(qgrad_rows, "seq", split_axis=1, concat_axis=2, tiled=True),
        lax.all_to_all(kgrad_rows, "seq", split_axis=1, concat_axis=2, tiled=True),
        lax.all_to_all(vgrad_rows, "seq", split_axis=1, concat_axis=2, tiled=True),
    )
    attended = (join_heads(space_out) + back_out.astype(jnp.float32)).astype(jnp.bfloat16)
    query_grad = (join_heads(space_grads[0]) + back_query.astype(jnp.float32)).astype(jnp.bfloat16)
    key_grad = (join_heads(space_grads[1]) + back_key.astype(jnp.float32)).astype(jnp.bfloat16)
    value_grad = (join_heads(space_grads[2]) + back_value.astype(jnp.float32)).astype(jnp.bfloat16)
    bias_part = jnp.tensordot(
        jnp.sum(time_grads[3], axis=(0, 1)),
        onehot,
        axes=((1, 2), (1, 2)),
        precision=lax.Precision.HIGHEST,
    )
    summed = lax.psum(bias_part, ("dp", "seq"))
    bias_grad = summed / math.sqrt(lax.axis_size("dp") * queries.shape[0] * frames_all * positions)
    return (attended, query_grad, key_grad, value_grad, bias_grad)


ROWS = 16
VMEM_BYTES = 60_000_000
MESH = pl.DeviceIdType.MESH
NT = (((1,), (1,)), ((), ()))
NN = (((1,), (0,)), ((), ()))
TN = (((0,), (0,)), ((), ()))


def dot(left, right, dims):
    return lax.dot_general(left, right, dims, preferred_element_type=jnp.float32)


def attend_block(query, key, value, slope, extra, scaling):
    scores = dot(query, key, NT) * scaling + extra
    share_grad = dot(slope, value, NT)
    weights = jnp.exp(scores - jnp.max(scores, axis=-1, keepdims=True))
    shares = weights * (1.0 / jnp.sum(weights, axis=-1, keepdims=True))
    shares_half = shares.astype(jnp.bfloat16)
    spread = jnp.sum(shares * share_grad, axis=-1, keepdims=True)
    score_grad = shares * (share_grad - spread)
    score_half = score_grad.astype(jnp.bfloat16)
    grads = (
        dot(shares_half, value, NN),
        dot(score_half, key, NN) * scaling,
        dot(score_half, query, TN) * scaling,
        dot(shares_half, slope, TN),
    )
    return grads, score_grad


def partner(count, me, off, back=False):
    if count & (count - 1):
        return lax.rem(me + (count - off if back else off), count)
    other, bit = 0, 1
    while bit < count:
        mine = lax.rem(me // bit, 2)
        other = other + bit * (1 - mine if off & bit else mine)
        bit *= 2
    return other


def kernel(
    dp, n, heads, bias_scale,
    q_ref, k_ref, v_ref, c_ref, count_ref, clip_ref, bias_ref,
    out_ref, qg_ref, kg_ref, vg_ref, bg_ref,
    held, rx, res, ret, space, done, bx, by,
    load_sem, own_sem, fs, fr, bs, br, xs, xr, ys, yr, ws,
):
    ins = (q_ref, k_ref, v_ref, c_ref)
    outs = (out_ref, qg_ref, kg_ref, vg_ref)
    rows, width = q_ref.shape
    size = width // heads
    per = heads // n
    scaling = 1.0 / math.sqrt(size)
    me = lax.axis_index("seq")
    me_dp = lax.axis_index("dp")

    def cols(index):
        return pl.ds(pl.multiple_of(index * size, size), size)

    def load(a):
        return pltpu.make_async_copy(ins[a], held.at[a], load_sem.at[a])

    def own(a):
        mine = pl.ds(pl.multiple_of(me * per * size, size), per * size)
        return pltpu.make_async_copy(ins[a].at[:, mine], rx.at[a, me], own_sem.at[a])

    def forth(r, a, off, slot):
        to = partner(n, me, off)
        return pltpu.make_async_remote_copy(
            src_ref=ins[a].at[:, cols(to * per + r)],
            dst_ref=rx.at[a, slot, :, cols(r)],
            send_sem=fs.at[r, a, off - 1],
            recv_sem=fr.at[r, a, off - 1],
            device_id={"seq": to},
            device_id_type=MESH,
        )

    def back(r, a, off, slot):
        to = partner(n, me, off)
        return pltpu.make_async_remote_copy(
            src_ref=res.at[a, to, :, cols(r)],
            dst_ref=ret.at[a, :, cols(slot * per + r)],
            send_sem=bs.at[r, a, off - 1],
            recv_sem=br.at[r, a, off - 1],
            device_id={"seq": to},
            device_id_type=MESH,
        )

    def bias_dp(off, slot):
        return pltpu.make_async_remote_copy(
            src_ref=bx.at[me_dp],
            dst_ref=bx.at[slot],
            send_sem=xs.at[off - 1],
            recv_sem=xr.at[off - 1],
            device_id={"dp": partner(dp, me_dp, off)},
            device_id_type=MESH,
        )

    def bias_seq(off, slot):
        return pltpu.make_async_remote_copy(
            src_ref=by.at[me],
            dst_ref=by.at[slot],
            send_sem=ys.at[off - 1],
            recv_sem=yr.at[off - 1],
            device_id={"seq": partner(n, me, off)},
            device_id_type=MESH,
        )

    for a in range(4):
        load(a).start()
        own(a).start()
    barrier = pltpu.get_barrier_semaphore()
    for off in range(1, n):
        pl.semaphore_signal(
            barrier, inc=1, device_id={"seq": partner(n, me, off)}, device_id_type=MESH
        )
    for off in range(1, dp):
        pl.semaphore_signal(
            barrier, inc=1, device_id={"dp": partner(dp, me_dp, off)}, device_id_type=MESH
        )
    pl.semaphore_wait(barrier, n - 1 + dp - 1)

    def send(r):
        for a in range(4):
            for off in range(n - 1, 0, -1):
                forth(r, a, off, me).start()

    for r in range(min(2, per)):
        send(r)

    def pairs_of(span):
        tokens = n * span
        row = lax.broadcasted_iota(jnp.int32, (tokens, tokens), 0)
        col = lax.broadcasted_iota(jnp.int32, (tokens, tokens), 1)
        row_frame, col_frame = row // span, col // span
        row_clip = jnp.zeros((tokens, tokens), jnp.int32)
        col_clip = jnp.zeros((tokens, tokens), jnp.int32)
        for f in range(n):
            row_clip = jnp.where(row_frame == f, clip_ref[0, f], row_clip)
            col_clip = jnp.where(col_frame == f, clip_ref[0, f], col_clip)
        same = row - row_frame * span == col - col_frame * span
        return jnp.abs(row_frame - col_frame), (row_clip == col_clip) & same

    wide = max(ROWS, 128 // n // ROWS * ROWS)
    spans = [(at, min(wide, rows - at)) for at in range(0, rows, wide)]
    pairs = {span: pairs_of(span) for _, span in spans}
    live = lax.broadcasted_iota(jnp.int32, (rows, rows), 1) < count_ref[0, 0]
    space_extra = jnp.where(live, 0.0, -1e30)
    lane = lax.broadcasted_iota(jnp.int32, (8, 128), 1)
    line = lax.broadcasted_iota(jnp.int32, (8, 128), 0)

    for a in range(4):
        load(a).wait()
        own(a).wait()
    bx[me_dp] = jnp.zeros((8, 128), jnp.float32)

    def spatial(h):
        parts = [held[a, :, cols(h)] for a in range(4)]
        grads, _ = attend_block(*parts, space_extra, scaling)
        for a in range(4):
            space[a, :, cols(h)] = grads[a]

    def temporal(r):
        head = me * per + r
        extras, totals = {}, {}
        for span, (distance, allowed) in pairs.items():
            bias = jnp.zeros(distance.shape, jnp.float32)
            for d in range(n):
                bias = jnp.where(distance == d, bias_ref[d, head], bias)
            extras[span] = jnp.where(allowed, bias, -1e30)
            totals[span] = jnp.zeros(distance.shape, jnp.float32)
        for at, span in spans:
            parts = [
                jnp.concatenate([rx[a, f, at : at + span, cols(r)] for f in range(n)], axis=0)
                for a in range(4)
            ]
            grads, score_grad = attend_block(*parts, extras[span], scaling)
            totals[span] = totals[span] + score_grad
            for a in range(4):
                half = grads[a].astype(jnp.bfloat16)
                for f in range(n):
                    res[a, f, at : at + span, cols(r)] = half[f * span : (f + 1) * span]
        tile = bx[me_dp]
        for d in range(n):
            part = jnp.zeros((1, 1), jnp.float32)
            for span, (distance, _) in pairs.items():
                one = jnp.sum(
                    jnp.where(distance == d, totals[span], 0.0), axis=1, keepdims=True
                )
                part = part + jnp.sum(one, axis=0, keepdims=True)
            tile = jnp.where((line == d) & (lane == head), part, tile)
        bx[me_dp] = tile

    def pair(i, _):
        for j in range(2):
            spatial(2 * i + j)
        return 0

    def step(r, _):
        for a in range(4):
            for off in range(1, n):
                forth(r, a, off, partner(n, me, off, True)).wait_recv()

        @pl.when(r + 2 < per)
        def _():
            send(r + 2)

        temporal(r)
        for a in range(4):
            for off in range(n - 1, 0, -1):
                back(r, a, off, me).start()
        return 0

    early = heads // 4
    lax.fori_loop(0, early, pair, 0)
    lax.fori_loop(0, per, step, 0)

    for off in range(1, dp):
        bias_dp(off, me_dp).start()

    lax.fori_loop(early, heads // 2, pair, 0)

    def write(r, a, off, source):
        where = cols(source * per + r)
        return pltpu.make_async_copy(
            done.at[a, :, where], outs[a].at[:, where], ws.at[r, a, off]
        )

    def finish(r, _):
        for a in range(4):
            where = cols(me * per + r)
            done[a, :, where] = (
                space[a, :, where] + res[a, me, :, cols(r)].astype(jnp.float32)
            ).astype(jnp.bfloat16)
            write(r, a, 0, me).start()
        for a in range(4):
            for off in range(1, n):
                source = partner(n, me, off, True)
                back(r, a, off, source).wait_recv()
                where = cols(source * per + r)
                done[a, :, where] = (
                    space[a, :, where] + ret[a, :, where].astype(jnp.float32)
                ).astype(jnp.bfloat16)
                write(r, a, off, source).start()
        return 0

    lax.fori_loop(0, per - 1, finish, 0)

    for off in range(1, dp):
        bias_dp(off, partner(dp, me_dp, off, True)).wait_recv()
    summed = bx[0]
    for g in range(1, dp):
        summed = summed + bx[g]
    by[me] = summed * bias_scale
    for off in range(1, n):
        bias_seq(off, me).start()

    finish(per - 1, 0)

    for off in range(1, n):
        bias_seq(off, partner(n, me, off, True)).wait_recv()
    joined = by[0]
    for s in range(1, n):
        joined = joined + by[s]
    bg_ref[...] = joined[0:n, 0:heads]

    def drain(r, _):
        for a in range(4):
            for off in range(1, n):
                forth(r, a, off, me).wait_send()
                back(r, a, off, me).wait_send()
                write(r, a, off, partner(n, me, off, True)).wait()
            write(r, a, 0, me).wait()
        return 0

    lax.fori_loop(0, per, drain, 0)
    for off in range(1, dp):
        bias_dp(off, me_dp).wait_send()
    for off in range(1, n):
        bias_seq(off, me).wait_send()


def hand_over(*refs):
    count = (len(refs) - 2) // 3
    sources, targets, stages = refs[:count], refs[count : 2 * count], refs[2 * count : 3 * count]
    into_sem, out_sem = refs[3 * count :]
    into, out = [], []
    for i in range(count):
        rows = sources[i].shape[0]
        cuts = 3 if rows % (3 * ROWS) == 0 else 1
        for cut in range(cuts):
            part = pl.ds(cut * rows // cuts, rows // cuts)
            stage = stages[i].at[part]
            into.append(pltpu.make_async_copy(sources[i].at[part], stage, into_sem.at[i, cut]))
            out.append(pltpu.make_async_copy(stage, targets[i].at[part], out_sem.at[i, cut]))
    for copy in into:
        copy.start()
    for here, there in zip(into, out):
        here.wait()
        there.start()
    for copy in out:
        copy.wait()


def fused(dp, n, queries, keys, values, cotangent, spatial_count, clip_ids, time_bias):
    shape = queries.shape
    rows, width = shape[2:]
    heads = time_bias.shape[0]
    per = heads // n
    flat = jax.ShapeDtypeStruct((rows, width), jnp.bfloat16)
    hbm = pl.BlockSpec(memory_space=pltpu.HBM)
    smem = pl.BlockSpec(memory_space=pltpu.SMEM)
    vmem = pl.BlockSpec(memory_space=pltpu.VMEM)
    dma = pltpu.SemaphoreType.DMA
    shapes = [flat] * 4 + [jax.ShapeDtypeStruct((n, heads), jnp.float32)]
    results = pl.pallas_call(
        functools.partial(kernel, dp, n, heads, 1.0 / math.sqrt(dp * n * rows)),
        out_shape=shapes,
        in_specs=[hbm] * 4 + [smem] * 3,
        out_specs=[hbm] * 4 + [vmem],
        scratch_shapes=[
            pltpu.VMEM((4, rows, width), jnp.bfloat16),
            pltpu.VMEM((4, n, rows, width // n), jnp.bfloat16),
            pltpu.VMEM((4, n, rows, width // n), jnp.bfloat16),
            pltpu.VMEM((4, rows, width), jnp.bfloat16),
            pltpu.VMEM((4, rows, width), jnp.float32),
            pltpu.VMEM((4, rows, width), jnp.bfloat16),
            pltpu.VMEM((dp, 8, 128), jnp.float32),
            pltpu.VMEM((n, 8, 128), jnp.float32),
            dma((4,)),
            dma((4,)),
            dma((per, 4, n - 1)),
            dma((per, 4, n - 1)),
            dma((per, 4, n - 1)),
            dma((per, 4, n - 1)),
            dma((dp - 1,)),
            dma((dp - 1,)),
            dma((n - 1,)),
            dma((n - 1,)),
            dma((per, 4, n)),
        ],
        compiler_params=pltpu.CompilerParams(
            collective_id=0, has_side_effects=True, vmem_limit_bytes=VMEM_BYTES
        ),
        name="space_time_attention",
    )(
        *(array.reshape(rows, width) for array in (queries, keys, values, cotangent)),
        spatial_count,
        clip_ids,
        time_bias.T,
    )
    results = pl.pallas_call(
        hand_over,
        out_shape=shapes,
        in_specs=[hbm] * 5,
        out_specs=[hbm] * 5,
        scratch_shapes=[pltpu.VMEM(kind.shape, kind.dtype) for kind in shapes]
        + [dma((5, 3)), dma((5, 3))],
        compiler_params=pltpu.CompilerParams(vmem_limit_bytes=VMEM_BYTES),
        name="hand_over",
    )(*results)
    return tuple(array.reshape(shape) for array in results[:4]) + (results[4].T,)


def on_mesh(dp, n, queries, *rest):
    groups, frames, rows, width = queries.shape
    heads = rest[-1].shape[0]
    fits = groups == 1 and frames == 1 and rows % ROWS == 0 and (width // heads) % 128 == 0
    if fits and heads <= 128 and n > 1 and dp > 1 and heads % n == 0 and heads % 2 == 0 and n <= 8:
        return fused(dp, n, queries, *rest)
    return on_device(queries, *rest)


def solution(mesh):
    return jax.shard_map(
        functools.partial(on_mesh, mesh.shape["dp"], mesh.shape["seq"]),
        mesh=mesh,
        in_specs=(
            P("dp", "seq", None, None),
            P("dp", "seq", None, None),
            P("dp", "seq", None, None),
            P("dp", "seq", None, None),
            P("dp", "seq"),
            P("dp", None),
            P(),
        ),
        out_specs=(
            P("dp", "seq", None, None),
            P("dp", "seq", None, None),
            P("dp", "seq", None, None),
            P("dp", "seq", None, None),
            P(),
        ),
        check_vma=False,
    )
```

```python
import functools
import math

import jax
import jax.numpy as jnp
from jax import lax
from jax.experimental import pallas as pl
from jax.experimental.pallas import tpu as pltpu
from jax.sharding import PartitionSpec as P

SPACE_PATTERNS = ("bfihe,bfjhe->bfhij", "bfhij,bfjhe->bfihe", "bfhij,bfihe->bfjhe")
TIME_PATTERNS = ("biphe,bjphe->bphij", "bphij,bjphe->biphe", "bphij,biphe->bjphe")


def split_heads(tensor, head_count):
    return tensor.reshape(tensor.shape[:-1] + (head_count, tensor.shape[-1] // head_count))


def join_heads(tensor):
    return tensor.reshape(tensor.shape[:-2] + (tensor.shape[-2] * tensor.shape[-1],))


def attend_forward(patterns, query_part, key_part, value_part, bias, allowed):
    scaling = 1.0 / math.sqrt(query_part.shape[-1])
    scores = (
        jnp.einsum(patterns[0], query_part, key_part, preferred_element_type=jnp.float32) * scaling
        + bias
    )
    scores = jnp.where(allowed, scores, -1e30)
    row_peak = jnp.max(scores, axis=-1, keepdims=True)
    weights = jnp.exp(scores - row_peak)
    shares = weights / jnp.sum(weights, axis=-1, keepdims=True)
    shares_half = shares.astype(jnp.bfloat16)
    result = jnp.einsum(patterns[1], shares_half, value_part, preferred_element_type=jnp.float32)
    return (shares, shares_half, result)


def attend_backward(
    patterns, query_part, key_part, value_part, cotangent_part, shares, shares_half
):
    scaling = 1.0 / math.sqrt(query_part.shape[-1])
    value_grad = jnp.einsum(
        patterns[2], shares_half, cotangent_part, preferred_element_type=jnp.float32
    )
    share_grad = jnp.einsum(
        patterns[0], cotangent_part, value_part, preferred_element_type=jnp.float32
    )
    spread = jnp.sum(shares * share_grad, axis=-1, keepdims=True)
    score_grad = shares * (share_grad - spread)
    score_half = score_grad.astype(jnp.bfloat16)
    query_grad = (
        jnp.einsum(patterns[1], score_half, key_part, preferred_element_type=jnp.float32) * scaling
    )
    key_grad = (
        jnp.einsum(patterns[2], score_half, query_part, preferred_element_type=jnp.float32)
        * scaling
    )
    return (query_grad, key_grad, value_grad, score_grad)


def on_device(queries, keys, values, cotangent, spatial_count, clip_ids, time_bias):
    head_count, frames_all = time_bias.shape
    positions = queries.shape[2]
    row_index = lax.broadcasted_iota(jnp.int32, (frames_all, frames_all), 0)
    col_index = lax.broadcasted_iota(jnp.int32, (frames_all, frames_all), 1)
    distance = jnp.abs(row_index - col_index)
    lag_index = lax.broadcasted_iota(jnp.int32, (frames_all, frames_all, frames_all), 0)
    onehot = (lag_index == distance[None]).astype(jnp.float32)
    bias_table = jnp.tensordot(time_bias, onehot, axes=1, precision=lax.Precision.HIGHEST)[
        None, None
    ]
    same_clip = (clip_ids[:, :, None] == clip_ids[:, None, :])[:, None, None]
    position = lax.broadcasted_iota(jnp.int32, (1, 1, 1, 1, positions), 4)
    live_keys = position < spatial_count[:, :, None, None, None]
    space_query = split_heads(queries, head_count)
    space_key = split_heads(keys, head_count)
    space_value = split_heads(values, head_count)
    space_slope = split_heads(cotangent, head_count)
    space_shares, space_half, space_out = attend_forward(
        SPACE_PATTERNS, space_query, space_key, space_value, 0.0, live_keys
    )
    space_grads = attend_backward(
        SPACE_PATTERNS, space_query, space_key, space_value, space_slope, space_shares, space_half
    )
    query_rows, key_rows, value_rows = (
        lax.all_to_all(queries, "seq", split_axis=2, concat_axis=1, tiled=True),
        lax.all_to_all(keys, "seq", split_axis=2, concat_axis=1, tiled=True),
        lax.all_to_all(values, "seq", split_axis=2, concat_axis=1, tiled=True),
    )
    query_part = split_heads(query_rows, head_count)
    key_part = split_heads(key_rows, head_count)
    value_part = split_heads(value_rows, head_count)
    shares, shares_half, result = attend_forward(
        TIME_PATTERNS, query_part, key_part, value_part, bias_table, same_clip
    )
    held = (query_part, key_part, value_part)
    back_out = lax.all_to_all(
        join_heads(result).astype(jnp.bfloat16), "seq", split_axis=1, concat_axis=2, tiled=True
    )
    slope_rows = lax.all_to_all(cotangent, "seq", split_axis=2, concat_axis=1, tiled=True)
    slope_part = split_heads(slope_rows, head_count)
    time_grads = attend_backward(
        TIME_PATTERNS, held[0], held[1], held[2], slope_part, shares, shares_half
    )
    qgrad_rows = join_heads(time_grads[0]).astype(jnp.bfloat16)
    kgrad_rows = join_heads(time_grads[1]).astype(jnp.bfloat16)
    vgrad_rows = join_heads(time_grads[2]).astype(jnp.bfloat16)
    back_query, back_key, back_value = (
        lax.all_to_all(qgrad_rows, "seq", split_axis=1, concat_axis=2, tiled=True),
        lax.all_to_all(kgrad_rows, "seq", split_axis=1, concat_axis=2, tiled=True),
        lax.all_to_all(vgrad_rows, "seq", split_axis=1, concat_axis=2, tiled=True),
    )
    attended = (join_heads(space_out) + back_out.astype(jnp.float32)).astype(jnp.bfloat16)
    query_grad = (join_heads(space_grads[0]) + back_query.astype(jnp.float32)).astype(jnp.bfloat16)
    key_grad = (join_heads(space_grads[1]) + back_key.astype(jnp.float32)).astype(jnp.bfloat16)
    value_grad = (join_heads(space_grads[2]) + back_value.astype(jnp.float32)).astype(jnp.bfloat16)
    bias_part = jnp.tensordot(
        jnp.sum(time_grads[3], axis=(0, 1)),
        onehot,
        axes=((1, 2), (1, 2)),
        precision=lax.Precision.HIGHEST,
    )
    summed = lax.psum(bias_part, ("dp", "seq"))
    bias_grad = summed / math.sqrt(lax.axis_size("dp") * queries.shape[0] * frames_all * positions)
    return (attended, query_grad, key_grad, value_grad, bias_grad)


ROWS = 16
VMEM_BYTES = 60_000_000
MESH = pl.DeviceIdType.MESH
NT = (((1,), (1,)), ((), ()))
NN = (((1,), (0,)), ((), ()))
TN = (((0,), (0,)), ((), ()))


def dot(left, right, dims):
    return lax.dot_general(left, right, dims, preferred_element_type=jnp.float32)


def attend_block(query, key, value, slope, extra, scaling):
    scores = dot(query, key, NT) * scaling + extra
    share_grad = dot(slope, value, NT)
    weights = jnp.exp(scores - jnp.max(scores, axis=-1, keepdims=True))
    shares = weights * (1.0 / jnp.sum(weights, axis=-1, keepdims=True))
    shares_half = shares.astype(jnp.bfloat16)
    spread = jnp.sum(shares * share_grad, axis=-1, keepdims=True)
    score_grad = shares * (share_grad - spread)
    score_half = score_grad.astype(jnp.bfloat16)
    grads = (
        dot(shares_half, value, NN),
        dot(score_half, key, NN) * scaling,
        dot(score_half, query, TN) * scaling,
        dot(shares_half, slope, TN),
    )
    return grads, score_grad


def partner(count, me, off, back=False):
    if count & (count - 1):
        return lax.rem(me + (count - off if back else off), count)
    other, bit = 0, 1
    while bit < count:
        mine = lax.rem(me // bit, 2)
        other = other + bit * (1 - mine if off & bit else mine)
        bit *= 2
    return other


def kernel(
    dp, n, heads, bias_scale,
    q_ref, k_ref, v_ref, c_ref, count_ref, clip_ref, bias_ref,
    out_ref, qg_ref, kg_ref, vg_ref, bg_ref,
    held, rx, res, ret, space, done, bx, by,
    load_sem, own_sem, fs, fr, bs, br, xs, xr, ys, yr, ws,
):
    ins = (q_ref, k_ref, v_ref, c_ref)
    outs = (out_ref, qg_ref, kg_ref, vg_ref)
    rows, width = q_ref.shape
    size = width // heads
    per = heads // n
    scaling = 1.0 / math.sqrt(size)
    me = lax.axis_index("seq")
    me_dp = lax.axis_index("dp")

    def cols(index):
        return pl.ds(pl.multiple_of(index * size, size), size)

    def load(a):
        return pltpu.make_async_copy(ins[a], held.at[a], load_sem.at[a])

    def own(a):
        mine = pl.ds(pl.multiple_of(me * per * size, size), per * size)
        return pltpu.make_async_copy(ins[a].at[:, mine], rx.at[a, me], own_sem.at[a])

    def forth(r, a, off, slot):
        to = partner(n, me, off)
        return pltpu.make_async_remote_copy(
            src_ref=ins[a].at[:, cols(to * per + r)],
            dst_ref=rx.at[a, slot, :, cols(r)],
            send_sem=fs.at[r, a, off - 1],
            recv_sem=fr.at[r, a, off - 1],
            device_id={"seq": to},
            device_id_type=MESH,
        )

    def back(r, a, off, slot):
        to = partner(n, me, off)
        return pltpu.make_async_remote_copy(
            src_ref=res.at[a, to, :, cols(r)],
            dst_ref=ret.at[a, :, cols(slot * per + r)],
            send_sem=bs.at[r, a, off - 1],
            recv_sem=br.at[r, a, off - 1],
            device_id={"seq": to},
            device_id_type=MESH,
        )

    def pass_on(way, s, slot):
        return pltpu.make_async_remote_copy(
            src_ref=bx.at[slot],
            dst_ref=bx.at[slot],
            send_sem=xs.at[way, s],
            recv_sem=xr.at[way, s],
            device_id={"dp": me_dp - 1 if way else me_dp + 1},
            device_id_type=MESH,
        )

    def line_step(s):
        @pl.when((me_dp < dp - 1) & (me_dp >= s))
        def _():
            pass_on(0, s, me_dp - s).start()

        @pl.when((me_dp > 0) & (me_dp + s < dp))
        def _():
            pass_on(1, s, me_dp + s).start()

        @pl.when(me_dp >= s + 1)
        def _():
            pass_on(0, s, me_dp - 1 - s).wait_recv()

        @pl.when(me_dp + 1 + s < dp)
        def _():
            pass_on(1, s, me_dp + 1 + s).wait_recv()

    def bias_seq(off, slot):
        return pltpu.make_async_remote_copy(
            src_ref=by.at[me],
            dst_ref=by.at[slot],
            send_sem=ys.at[off - 1],
            recv_sem=yr.at[off - 1],
            device_id={"seq": partner(n, me, off)},
            device_id_type=MESH,
        )

    for a in range(4):
        load(a).start()
        own(a).start()
    barrier = pltpu.get_barrier_semaphore()
    for off in range(1, n):
        pl.semaphore_signal(
            barrier, inc=1, device_id={"seq": partner(n, me, off)}, device_id_type=MESH
        )
    for there, step_to in ((me_dp > 0, -1), (me_dp < dp - 1, 1)):

        @pl.when(there)
        def _():
            pl.semaphore_signal(
                barrier, inc=1, device_id={"dp": me_dp + step_to}, device_id_type=MESH
            )

    ends = 1 // (me_dp + 1) + (me_dp + 1) // dp
    pl.semaphore_wait(barrier, n + 1 - ends)

    def send(r):
        for a in range(4):
            for off in range(n - 1, 0, -1):
                forth(r, a, off, me).start()

    for r in range(min(2, per)):
        send(r)

    def pairs_of(span):
        tokens = n * span
        row = lax.broadcasted_iota(jnp.int32, (tokens, tokens), 0)
        col = lax.broadcasted_iota(jnp.int32, (tokens, tokens), 1)
        row_frame, col_frame = row // span, col // span
        row_clip = jnp.zeros((tokens, tokens), jnp.int32)
        col_clip = jnp.zeros((tokens, tokens), jnp.int32)
        for f in range(n):
            row_clip = jnp.where(row_frame == f, clip_ref[0, f], row_clip)
            col_clip = jnp.where(col_frame == f, clip_ref[0, f], col_clip)
        same = row - row_frame * span == col - col_frame * span
        return jnp.abs(row_frame - col_frame), (row_clip == col_clip) & same

    wide = max(ROWS, 128 // n // ROWS * ROWS)
    spans = [(at, min(wide, rows - at)) for at in range(0, rows, wide)]
    pairs = {span: pairs_of(span) for _, span in spans}
    live = lax.broadcasted_iota(jnp.int32, (rows, rows), 1) < count_ref[0, 0]
    space_extra = jnp.where(live, 0.0, -1e30)
    lane = lax.broadcasted_iota(jnp.int32, (8, 128), 1)
    line = lax.broadcasted_iota(jnp.int32, (8, 128), 0)

    for a in range(4):
        load(a).wait()
        own(a).wait()
    bx[me_dp] = jnp.zeros((8, 128), jnp.float32)

    def spatial(h):
        parts = [held[a, :, cols(h)] for a in range(4)]
        grads, _ = attend_block(*parts, space_extra, scaling)
        for a in range(4):
            space[a, :, cols(h)] = grads[a]

    def temporal(r):
        head = me * per + r
        extras, totals = {}, {}
        for span, (distance, allowed) in pairs.items():
            bias = jnp.zeros(distance.shape, jnp.float32)
            for d in range(n):
                bias = jnp.where(distance == d, bias_ref[d, head], bias)
            extras[span] = jnp.where(allowed, bias, -1e30)
            totals[span] = jnp.zeros(distance.shape, jnp.float32)
        for at, span in spans:
            parts = [
                jnp.concatenate([rx[a, f, at : at + span, cols(r)] for f in range(n)], axis=0)
                for a in range(4)
            ]
            grads, score_grad = attend_block(*parts, extras[span], scaling)
            totals[span] = totals[span] + score_grad
            for a in range(4):
                half = grads[a].astype(jnp.bfloat16)
                for f in range(n):
                    res[a, f, at : at + span, cols(r)] = half[f * span : (f + 1) * span]
        tile = bx[me_dp]
        for d in range(n):
            part = jnp.zeros((1, 1), jnp.float32)
            for span, (distance, _) in pairs.items():
                one = jnp.sum(
                    jnp.where(distance == d, totals[span], 0.0), axis=1, keepdims=True
                )
                part = part + jnp.sum(one, axis=0, keepdims=True)
            tile = jnp.where((line == d) & (lane == head), part, tile)
        bx[me_dp] = tile

    def pair(i, _):
        for j in range(2):
            spatial(2 * i + j)
        return 0

    def step(r, _):
        for a in range(4):
            for off in range(1, n):
                forth(r, a, off, partner(n, me, off, True)).wait_recv()

        @pl.when(r + 2 < per)
        def _():
            send(r + 2)

        temporal(r)
        for a in range(4):
            for off in range(n - 1, 0, -1):
                back(r, a, off, me).start()
        return 0

    early = heads // 4
    lax.fori_loop(0, early, pair, 0)
    lax.fori_loop(0, per, step, 0)

    lax.fori_loop(early, heads // 2, pair, 0)

    def write(r, a, off, source):
        where = cols(source * per + r)
        return pltpu.make_async_copy(
            done.at[a, :, where], outs[a].at[:, where], ws.at[r, a, off]
        )

    def finish(r, _):
        for a in range(4):
            where = cols(me * per + r)
            done[a, :, where] = (
                space[a, :, where] + res[a, me, :, cols(r)].astype(jnp.float32)
            ).astype(jnp.bfloat16)
            write(r, a, 0, me).start()
        for a in range(4):
            for off in range(1, n):
                source = partner(n, me, off, True)
                back(r, a, off, source).wait_recv()
                where = cols(source * per + r)
                done[a, :, where] = (
                    space[a, :, where] + ret[a, :, where].astype(jnp.float32)
                ).astype(jnp.bfloat16)
                write(r, a, off, source).start()
        return 0

    half = (dp - 1) // 2
    for s in range(half):
        line_step(s)
    lax.fori_loop(0, per - 1, finish, 0)
    for s in range(half, dp - 1):
        line_step(s)
    summed = bx[0]
    for g in range(1, dp):
        summed = summed + bx[g]
    by[me] = summed * bias_scale
    for off in range(1, n):
        bias_seq(off, me).start()

    finish(per - 1, 0)

    for off in range(1, n):
        bias_seq(off, partner(n, me, off, True)).wait_recv()
    joined = by[0]
    for s in range(1, n):
        joined = joined + by[s]
    bg_ref[...] = joined[0:n, 0:heads]

    def drain(r, _):
        for a in range(4):
            for off in range(1, n):
                forth(r, a, off, me).wait_send()
                back(r, a, off, me).wait_send()
                write(r, a, off, partner(n, me, off, True)).wait()
            write(r, a, 0, me).wait()
        return 0

    lax.fori_loop(0, per, drain, 0)
    for s in range(dp - 1):

        @pl.when((me_dp < dp - 1) & (me_dp >= s))
        def _():
            pass_on(0, s, me_dp - s).wait_send()

        @pl.when((me_dp > 0) & (me_dp + s < dp))
        def _():
            pass_on(1, s, me_dp + s).wait_send()

    for off in range(1, n):
        bias_seq(off, me).wait_send()


def hand_over(*refs):
    count = (len(refs) - 2) // 3
    sources, targets, stages = refs[:count], refs[count : 2 * count], refs[2 * count : 3 * count]
    into_sem, out_sem = refs[3 * count :]
    into, out = [], []
    for i in range(count):
        rows = sources[i].shape[0]
        cuts = 3 if rows % (3 * ROWS) == 0 else 1
        for cut in range(cuts):
            part = pl.ds(cut * rows // cuts, rows // cuts)
            stage = stages[i].at[part]
            into.append(pltpu.make_async_copy(sources[i].at[part], stage, into_sem.at[i, cut]))
            out.append(pltpu.make_async_copy(stage, targets[i].at[part], out_sem.at[i, cut]))
    for copy in into:
        copy.start()
    for here, there in zip(into, out):
        here.wait()
        there.start()
    for copy in out:
        copy.wait()


def fused(dp, n, queries, keys, values, cotangent, spatial_count, clip_ids, time_bias):
    shape = queries.shape
    rows, width = shape[2:]
    heads = time_bias.shape[0]
    per = heads // n
    flat = jax.ShapeDtypeStruct((rows, width), jnp.bfloat16)
    hbm = pl.BlockSpec(memory_space=pltpu.HBM)
    smem = pl.BlockSpec(memory_space=pltpu.SMEM)
    vmem = pl.BlockSpec(memory_space=pltpu.VMEM)
    dma = pltpu.SemaphoreType.DMA
    shapes = [flat] * 4 + [jax.ShapeDtypeStruct((n, heads), jnp.float32)]
    results = pl.pallas_call(
        functools.partial(kernel, dp, n, heads, 1.0 / math.sqrt(dp * n * rows)),
        out_shape=shapes,
        in_specs=[hbm] * 4 + [smem] * 3,
        out_specs=[hbm] * 4 + [vmem],
        scratch_shapes=[
            pltpu.VMEM((4, rows, width), jnp.bfloat16),
            pltpu.VMEM((4, n, rows, width // n), jnp.bfloat16),
            pltpu.VMEM((4, n, rows, width // n), jnp.bfloat16),
            pltpu.VMEM((4, rows, width), jnp.bfloat16),
            pltpu.VMEM((4, rows, width), jnp.float32),
            pltpu.VMEM((4, rows, width), jnp.bfloat16),
            pltpu.VMEM((dp, 8, 128), jnp.float32),
            pltpu.VMEM((n, 8, 128), jnp.float32),
            dma((4,)),
            dma((4,)),
            dma((per, 4, n - 1)),
            dma((per, 4, n - 1)),
            dma((per, 4, n - 1)),
            dma((per, 4, n - 1)),
            dma((2, dp - 1)),
            dma((2, dp - 1)),
            dma((n - 1,)),
            dma((n - 1,)),
            dma((per, 4, n)),
        ],
        compiler_params=pltpu.CompilerParams(
            collective_id=0, has_side_effects=True, vmem_limit_bytes=VMEM_BYTES
        ),
        name="space_time_attention",
    )(
        *(array.reshape(rows, width) for array in (queries, keys, values, cotangent)),
        spatial_count,
        clip_ids,
        time_bias.T,
    )
    results = pl.pallas_call(
        hand_over,
        out_shape=shapes,
        in_specs=[hbm] * 5,
        out_specs=[hbm] * 5,
        scratch_shapes=[pltpu.VMEM(kind.shape, kind.dtype) for kind in shapes]
        + [dma((5, 3)), dma((5, 3))],
        compiler_params=pltpu.CompilerParams(vmem_limit_bytes=VMEM_BYTES),
        name="hand_over",
    )(*results)
    return tuple(array.reshape(shape) for array in results[:4]) + (results[4].T,)


def on_mesh(dp, n, queries, *rest):
    groups, frames, rows, width = queries.shape
    heads = rest[-1].shape[0]
    fits = groups == 1 and frames == 1 and rows % ROWS == 0 and (width // heads) % 128 == 0
    if fits and heads <= 128 and n > 1 and dp > 1 and heads % n == 0 and heads % 2 == 0 and n <= 8:
        return fused(dp, n, queries, *rest)
    return on_device(queries, *rest)


def solution(mesh):
    return jax.shard_map(
        functools.partial(on_mesh, mesh.shape["dp"], mesh.shape["seq"]),
        mesh=mesh,
        in_specs=(
            P("dp", "seq", None, None),
            P("dp", "seq", None, None),
            P("dp", "seq", None, None),
            P("dp", "seq", None, None),
            P("dp", "seq"),
            P("dp", None),
            P(),
        ),
        out_specs=(
            P("dp", "seq", None, None),
            P("dp", "seq", None, None),
            P("dp", "seq", None, None),
            P("dp", "seq", None, None),
            P(),
        ),
        check_vma=False,
    )
```
